32 devices in a mesh: row: 4 (over z), col: 8 (over y, x, core).
Axes of the slice: x: 2, y: 2, z: 4, core: 2. Of those that a mesh axis runs over, the one named last changes fastest.
Arguments:
- mask_field: float32 [1536, 3072], P('row', 'col'), may hold values from -1 to 1
- resist_goal: float32 [1536, 3072], P('row', 'col'), may hold values from 0 to 1
- kernels: float32 [8, 2, 64, 64], replicated, may hold values from -30 to 30
- colour: int32 [4, 8], P('row', 'col'), may hold values from 0 to 3
- active: int32 [4, 8], P('row', 'col'), may hold values 0 or 1
Outputs:
- final_mask: float32 [1536, 3072], P('row', 'col')
- next_tiles: float32 [2048, 4096], P('row', 'col')
The draws below stay inside these ranges and needn't reach their ends.
Inputs may be any that keep to these rules, and one draw needn't show every extreme that they name: Every entry of `colour` is 0, 1, 2 or 3, and neighbouring tiles may have the same colour.
All inputs are finite; a program needn't handle non-finite values. No bound on the sum of `active` on one device may be relied on, other than what follows from the above.
Results may differ from the reference program's by a relative error of at most 0.0035.
Values may be sent and summed in bfloat16 or wider, within the bound.
A program may use at most 64 MiB of HBM per device.

```python
import math
import jax
import jax.numpy as jnp
from jax import lax

TILE = 512
HALO = 64
FREQS = 64
KERN = 8
ITERS = 2
CORE = 384
NR = 1536
NC = 3072
N_ROW = 4
N_COL = 8


def set_ends(array, own_key, low, top_value):
    longest = array.shape.index(max(array.shape))
    spots = []
    for shift in (0, 1):
        where = [jax.random.randint(jax.random.fold_in(own_key, axis), (), 0, length) for axis, length in enumerate(array.shape)]
        where[longest] = (where[longest] + shift) % array.shape[longest]
        spots.append(tuple(where))
    return array.at[spots[0]].set(low).at[spots[1]].set(top_value)


def levels(stream_key, shape, shards, least, largest):
    def one(axis_at, shards_of):
        steps = jax.random.uniform(jax.random.fold_in(jax.random.fold_in(stream_key, 6), axis_at), (shards_of,), jnp.float32, least / len(shards), largest / len(shards))
        return jnp.repeat(jnp.exp(steps), shape[axis_at] // shards_of).reshape((-1,) + (1,) * (len(shape) - axis_at - 1))

    level = one(*shards[0])
    for cut in shards[1:]:
        level = level * one(*cut)
    return level


def bell_draw(rng, extent, width, bound, held_as=jnp.bfloat16):
    values = jax.random.normal(rng, extent, jnp.float32) * width
    return jnp.minimum(jnp.maximum(values, -bound), bound).astype(held_as)


def setup_inputs(seed: int = 0) -> dict:
    streams_of = jax.random.split(jax.random.key(seed), 6)
    mask_field = jnp.clip(jax.random.uniform(streams_of[0], (NR, NC), jnp.float32, -1.0, 1.0) * levels(streams_of[0], (NR, NC), ((0, 4), (1, 8)), -0.4, 0.0), -1.0, 1.0)
    resist_goal = jnp.clip(1.0 * jax.random.uniform(streams_of[1], (NR, NC), jnp.float32) ** levels(streams_of[1], (NR, NC), ((0, 4), (1, 8)), -0.2, 0.2), 0.0, 1.0)
    kernels = bell_draw(streams_of[2], (KERN, 2, FREQS, FREQS), (0.625 * TILE / FREQS), 30.0, jnp.float32)
    colour = set_ends(jax.random.randint(streams_of[3], (N_ROW, N_COL), 0, 4), jax.random.fold_in(streams_of[3], 1), 0, 3).astype(jnp.int32)
    active = set_ends((jax.random.randint(streams_of[4], (N_ROW, N_COL), 0, 4) < 3).astype(jnp.int32), jax.random.fold_in(streams_of[4], 1), 0, 1)
    return dict(mask_field=mask_field, resist_goal=resist_goal, kernels=kernels, colour=colour, active=active)


STEP_SIZE = 0.05
STEEPNESS = 4.0
THRESHOLD = 1.0

def make_tables(tile_len, freq_count):
    position = jnp.arange(tile_len, dtype=jnp.int32)
    frequency = jnp.arange(freq_count, dtype=jnp.int32) - freq_count // 2
    phases = frequency[:, None] * position[None, :] % tile_len
    angles = phases.astype(jnp.float32) * (2.0 * math.pi / tile_len)
    cosine = jnp.cos(angles)
    sine_part = jnp.sin(angles)
    forward_table = (jnp.concatenate([cosine, sine_part], 0).T / tile_len).astype(jnp.bfloat16)
    inverse_table = jnp.concatenate([cosine, sine_part], 0).T.astype(jnp.bfloat16)
    return (forward_table, cosine / tile_len, sine_part / tile_len, cosine, sine_part, inverse_table)

def tile_loss(extended, goal_block, kernels, tables):
    forward_table, cos_fwd, sin_fwd, cos_inv, sin_inv, inverse_table = tables
    freq_count = cos_fwd.shape[0]
    tile_len = extended.shape[0]
    core_len = goal_block.shape[0]
    halo_width = (tile_len - core_len) // 2
    highest = lax.Precision.HIGHEST
    partial_value = jnp.dot(extended.astype(jnp.bfloat16), forward_table, preferred_element_type=jnp.float32)
    part_cos = partial_value[:, :freq_count]
    part_sin = partial_value[:, freq_count:]
    spec_real = jnp.dot(cos_fwd, part_cos, precision=highest) - jnp.dot(sin_fwd, part_sin, precision=highest)
    spec_imag = -(jnp.dot(cos_fwd, part_sin, precision=highest) + jnp.dot(sin_fwd, part_cos, precision=highest))
    kern_real = kernels[:, 0]
    kern_imag = kernels[:, 1]
    filt_real = kern_real * spec_real - kern_imag * spec_imag
    filt_imag = kern_real * spec_imag + kern_imag * spec_real
    half_real = jnp.einsum('kab,by->kay', filt_real, cos_inv, precision=highest) - jnp.einsum('kab,by->kay', filt_imag, sin_inv, precision=highest)
    half_imag = jnp.einsum('kab,by->kay', filt_real, sin_inv, precision=highest) + jnp.einsum('kab,by->kay', filt_imag, cos_inv, precision=highest)
    upper_half = jnp.stack([half_real, half_imag], 1)
    lower_half = jnp.stack([-half_imag, half_real], 1)
    stacked = jnp.concatenate([upper_half, lower_half], 2)
    stacked = jnp.transpose(stacked, (2, 0, 1, 3)).reshape(2 * freq_count, -1).astype(jnp.bfloat16)
    fields = jnp.dot(inverse_table, stacked, preferred_element_type=jnp.float32)
    fields = fields.reshape(tile_len, -1, tile_len)
    intensity = lax.optimization_barrier(jnp.sum(fields * fields, axis=1))
    resist = jax.nn.sigmoid(STEEPNESS * (intensity - THRESHOLD))
    inner_part = resist[halo_width:halo_width + core_len, halo_width:halo_width + core_len]
    differ = inner_part - goal_block
    return jnp.sum(differ * differ)

def tile_gradient(extended, goal_block, kernels, tables):
    loss_value, pullback = jax.vjp(lambda pixels: tile_loss(pixels, goal_block, kernels, tables), extended)
    return pullback(jnp.ones_like(loss_value))[0]

def reference(mask_field, resist_goal, kernels, colour, active):
    tables = make_tables(TILE, FREQS)
    update_tiles = (colour == 0).astype(jnp.float32)
    update_pixels = jnp.repeat(jnp.repeat(update_tiles, CORE, axis=0), CORE, axis=1)
    weights = active.astype(jnp.float32)
    current = mask_field
    for iteration in range(ITERS):
        padded = jnp.pad(current, HALO)

        def add_tile(tile_index, summed):
            row_at = (tile_index // N_COL).astype(jnp.int32)
            col_at = (tile_index % N_COL).astype(jnp.int32)
            top_row = (row_at * CORE).astype(jnp.int32)
            left_col = (col_at * CORE).astype(jnp.int32)
            extended = lax.dynamic_slice(padded, (top_row, left_col), (TILE, TILE))
            goal_block = lax.dynamic_slice(resist_goal, (top_row, left_col), (CORE, CORE))
            gradient = tile_gradient(extended, goal_block, kernels, tables) * weights[row_at, col_at]
            window = lax.dynamic_slice(summed, (top_row, left_col), (TILE, TILE))
            return lax.dynamic_update_slice(summed, window + gradient, (top_row, left_col))
        summed = lax.fori_loop(0, N_ROW * N_COL, add_tile, jnp.zeros_like(padded))
        gradient = summed[HALO:HALO + N_ROW * CORE, HALO:HALO + N_COL * CORE]
        current = jnp.clip(current - STEP_SIZE * update_pixels * gradient, -1.0, 1.0)
    padded = jnp.pad(current, HALO)

    def place_tile(tile_index, output):
        row_at = (tile_index // N_COL).astype(jnp.int32)
        col_at = (tile_index % N_COL).astype(jnp.int32)
        extended = lax.dynamic_slice(padded, ((row_at * CORE).astype(jnp.int32), (col_at * CORE).astype(jnp.int32)), (TILE, TILE))
        return lax.dynamic_update_slice(output, extended, ((row_at * TILE).astype(jnp.int32), (col_at * TILE).astype(jnp.int32)))
    next_tiles = lax.fori_loop(0, N_ROW * N_COL, place_tile, jnp.zeros((N_ROW * TILE, N_COL * TILE), jnp.float32))
    return (current, next_tiles)
```

```python
import functools
import math

import jax
import jax.numpy as jnp
import numpy as np
from jax import lax
from jax.experimental import pallas as pl
from jax.experimental.pallas import tpu as pltpu
from jax.sharding import PartitionSpec as P

HALO = 64
FREQS = 64
ITERS = 2
STEP_SIZE = 0.05
STEEPNESS = 4.0
THRESHOLD = 1.0
YBLOCK = 64

DIRS = [(di, dj) for di in (0, 1, -1) for dj in (0, 1, -1) if (di, dj) != (0, 0)]


def slot(di, dj):
    return 3 * (di % 3) + dj % 3


def make_tables(core, tile):
    bf16 = jnp.bfloat16
    place = (np.arange(tile) + HALO) % tile
    frequency = np.arange(FREQS) - FREQS // 2

    def waves(position):
        angle = (frequency[None, :] * position[:, None] % tile) * (2.0 * math.pi / tile)
        return np.concatenate([np.cos(angle), np.sin(angle)], 1)

    whole = waves(place).astype(np.float32)
    high = whole.astype(bf16)
    low = (whole - high.astype(np.float32)).astype(bf16)
    below = waves(place - core) * (place >= core)[:, None]
    above = waves(place + core) * (place < 2 * HALO)[:, None]
    spread = np.concatenate([whole, below, above], 1).astype(np.float32)
    return dict(
        forward=np.ascontiguousarray((whole / tile).T).astype(bf16),
        whole=whole,
        half=np.concatenate([high[:core], low[:core], high[:core]], 1),
        inverse_t=np.ascontiguousarray(high[:core].T),
        inverse=high[:core],
        half_t=np.ascontiguousarray(np.concatenate([high[:core], low[:core]], 1).T),
        rows=spread.astype(bf16),
        cols=np.ascontiguousarray((spread / tile).T).astype(bf16),
    )


def kernel(
    axes,
    mask_ref,
    goal_ref,
    kern_ref,
    colour_ref,
    active_ref,
    forward_ref,
    whole_ref,
    half_ref,
    inverse_t_ref,
    inverse_ref,
    half_t_ref,
    rows_ref,
    cols_ref,
    final_ref,
    next_ref,
    mask16,
    vert16,
    side16,
    vert32,
    side32,
    window,
    image,
    grads,
    blocks,
    ka,
    kc,
    goal_t,
    weights,
    halfway,
    d_half,
    send_sems,
    recv_sems,
):
    core = mask_ref.shape[0]
    tile = core + 2 * HALO
    kerns = ka.shape[0]
    f32, bf16 = jnp.float32, jnp.bfloat16
    n_row, n_col = lax.axis_size(axes[0]), lax.axis_size(axes[1])
    row, col = lax.axis_index(axes[0]), lax.axis_index(axes[1])

    def exists(di, dj):
        there = (row + di >= 0) & (row + di < n_row)
        return there & (col + dj >= 0) & (col + dj < n_col)

    barrier = pltpu.get_barrier_semaphore()
    for di, dj in DIRS:

        @pl.when(exists(di, dj))
        def _(di=di, dj=dj):
            pl.semaphore_signal(
                barrier, inc=1, device_id=(row + di, col + dj), device_id_type=pl.DeviceIdType.MESH
            )

    def halo_refs(di, dj, source, vert, side):
        rows = {0: pl.ds(0, core), 1: pl.ds(core - HALO, HALO), -1: pl.ds(0, HALO)}[di]
        if dj == 0:
            return source.at[rows, :], vert.at[1 if di == 1 else 0]
        cols = pl.ds(core - 128, 128) if dj == 1 else pl.ds(0, 128)
        land = {0: pl.ds(0, core), 1: pl.ds(core + HALO, HALO), -1: pl.ds(core, HALO)}[di]
        return source.at[rows, cols], side.at[1 if dj == 1 else 0, land, :]

    def message(phase, di, dj, target):
        if phase < 2:
            pair = (mask16, vert16, side16) if phase == 0 else (mask_ref, vert32, side32)
            source, land = halo_refs(di, dj, *pair)
        else:
            source, land = grads.at[phase - 2, 0], grads.at[phase - 2, slot(-di, -dj)]
        return pltpu.make_async_remote_copy(
            src_ref=source,
            dst_ref=land,
            send_sem=send_sems.at[phase, slot(di, dj)],
            recv_sem=recv_sems.at[phase, slot(di, dj)],
            device_id=target,
            device_id_type=pl.DeviceIdType.MESH,
        )

    def send(phase):
        for di, dj in DIRS:

            @pl.when(exists(di, dj))
            def _(di=di, dj=dj):
                message(phase, di, dj, (row + di, col + dj)).start()

    def wait_arrivals(phase):
        for di, dj in DIRS:

            @pl.when(exists(-di, -dj))
            def _(di=di, dj=dj):
                message(phase, di, dj, (row - di, col - dj)).wait_recv()

    def wait_sent(phase):
        for di, dj in DIRS:

            @pl.when(exists(di, dj))
            def _(di=di, dj=dj):
                message(phase, di, dj, (row + di, col + dj)).wait_send()

    mask16[...] = mask_ref[...].astype(bf16)
    for di, dj in DIRS:

        @pl.when(jnp.logical_not(exists(di, dj)))
        def _(di=di, dj=dj):
            for vert, side in ((vert16, side16), (vert32, side32)):
                _, land = halo_refs(-di, -dj, mask_ref, vert, side)
                land[...] = jnp.zeros(land.shape, land.dtype)
            for step in range(ITERS):
                spot = grads.at[step, slot(di, dj)]
                spot[...] = jnp.zeros(spot.shape, spot.dtype)

    peers = sum(exists(di, dj).astype(jnp.int32) for di, dj in DIRS)
    pl.semaphore_wait(barrier, peers)

    send(0)
    send(1)

    goal_t[...] = goal_ref[...].T
    for k in range(kerns):
        real, imag = kern_ref[k, :FREQS, :], kern_ref[k, FREQS:, :]
        ka[k] = jnp.concatenate([real, -imag], 0).T
        kc[k] = jnp.concatenate([imag, real], 0).T
    update = jnp.where(colour_ref[0, 0] == 0, 1.0, 0.0).astype(f32)
    active = active_ref[0, 0].astype(f32)
    left_half = lax.broadcasted_iota(jnp.int32, (1, 128), 1) < FREQS
    for step in range(ITERS):
        grads[step, 0, FREQS:, :] = jnp.full((16, 128), update, f32).astype(bf16)

    image[:core, :core] = mask16[...]
    window[:core, :core] = mask_ref[...]

    for step in range(ITERS):
        if step == 0:
            wait_arrivals(0)
            image[core : core + HALO, :core] = vert16[0]
            image[core + HALO :, :core] = vert16[1]
            image[:, core:] = jnp.where(
                left_half, side16[0].astype(f32), side16[1].astype(f32)
            ).astype(bf16)
        else:
            image[...] = window[...].astype(bf16)

        partial = lax.dot_general(
            forward_ref[...], image[...], (((1,), (1,)), ((), ())), preferred_element_type=f32
        )
        quads = jnp.dot(
            partial, whole_ref[...], precision=lax.Precision.HIGHEST, preferred_element_type=f32
        ) * (1.0 / tile)
        upper, lower = quads[:FREQS], quads[FREQS:]
        real = upper - pltpu.roll(lower, FREQS, 1)
        imag = -(lower + pltpu.roll(upper, FREQS, 1))
        real = jnp.where(left_half, real, pltpu.roll(real, FREQS, 1))
        imag = jnp.where(left_half, imag, pltpu.roll(imag, FREQS, 1))

        for k in range(kerns):
            x = ka[k] * real - kc[k] * imag
            y = kc[k] * real + ka[k] * imag
            both = jnp.concatenate([jnp.concatenate([x, -y], 0), jnp.concatenate([y, x], 0)], 1)
            high = both.astype(bf16)
            at = pl.ds(k * 256, 256)
            weights[:128, at] = high
            weights[128:256, at] = high
            weights[256:, at] = (both - high.astype(f32)).astype(bf16)
        halfway[...] = jnp.dot(half_ref[...], weights[...], preferred_element_type=f32).astype(bf16)

        def rows_of_y(block, carry):
            at = pl.ds(pl.multiple_of(block * YBLOCK, YBLOCK), YBLOCK)
            stacked = jnp.concatenate(
                [halfway[at, kp * 128 : (kp + 1) * 128] for kp in range(2 * kerns)], 0
            )
            fields = jnp.dot(stacked, inverse_t_ref[...], preferred_element_type=f32)
            fields = fields.reshape(2 * kerns, YBLOCK, core)
            intensity = jnp.sum(fields * fields, axis=0)
            resist = 1.0 / (1.0 + jnp.exp(-STEEPNESS * (intensity - THRESHOLD)))
            slope = (4.0 * STEEPNESS) * (resist - goal_t[at, :]) * (resist * (1.0 - resist))
            d_fields = (fields * slope[None]).astype(bf16).reshape(2 * kerns * YBLOCK, core)
            back = jnp.dot(d_fields, inverse_ref[...], preferred_element_type=f32).astype(bf16)
            for kp in range(2 * kerns):
                d_half[at, kp * 128 : (kp + 1) * 128] = back[kp * YBLOCK : (kp + 1) * YBLOCK]
            return carry

        lax.fori_loop(0, core // YBLOCK, rows_of_y, 0)

        d_weights = jnp.dot(half_t_ref[...], d_half[...], preferred_element_type=f32)
        d_weights = d_weights[:128] + d_weights[128:]
        d_real = jnp.zeros((FREQS, 128), f32)
        d_imag = jnp.zeros((FREQS, 128), f32)
        for k in range(kerns):
            at = k * 256
            dx = d_weights[:FREQS, at : at + 128] + d_weights[FREQS:, at + 128 : at + 256]
            dy = d_weights[:FREQS, at + 128 : at + 256] - d_weights[FREQS:, at : at + 128]
            d_real += ka[k] * dx + kc[k] * dy
            d_imag += ka[k] * dy - kc[k] * dx
        d_real = d_real + pltpu.roll(d_real, FREQS, 1)
        d_imag = d_imag + pltpu.roll(d_imag, FREQS, 1)
        own = jnp.where(left_half, d_real, -d_imag) * (active * (1.0 / tile))
        grads[step, 0, :FREQS, :] = own.astype(bf16)
        send(2 + step)
        if step == 0:
            wait_arrivals(1)
            window[core : core + HALO, :core] = vert32[0]
            window[core + HALO :, :core] = vert32[1]
            window[:, core:] = jnp.where(left_half, side32[0], side32[1])
        wait_arrivals(2 + step)

        for gi in range(3):
            for gj in range(3):
                top = grads[step, 3 * gi + gj, :FREQS, :].astype(f32)
                turned = pltpu.roll(top, FREQS, 1)
                low = jnp.where(left_half, turned, -turned)
                blocks[gj * 128 : gj * 128 + 128, gi * 128 : gi * 128 + 128] = jnp.concatenate(
                    [top, low], 0
                ).astype(bf16)
        spread = lax.dot_general(
            rows_ref[...], blocks[...], (((1,), (1,)), ((), ())), preferred_element_type=f32
        ).astype(bf16)
        total = jnp.dot(spread, cols_ref[...], preferred_element_type=f32)

        bands = ((0, core), (core, HALO), (core + HALO, HALO))
        for gi, (start, size) in enumerate(bands):
            flags = [grads[step, 3 * gi + gj, FREQS : FREQS + 16, :].astype(f32)[:1] for gj in range(3)]
            scale = jnp.concatenate(
                [flags[0]] * (core // 128) + [jnp.where(left_half, flags[1], flags[2])], 1
            )
            at = slice(start, start + size)
            fresh = jnp.clip(window[at, :] - STEP_SIZE * scale * total[at], -1.0, 1.0)
            if step < ITERS - 1:
                window[at, :] = fresh
            else:
                if gi == 0:
                    final_ref[...] = fresh[:, :core]
                out = (start + HALO) % tile
                next_ref[out : out + size, :] = pltpu.roll(fresh, HALO, 1)

    for phase in range(2 + ITERS):
        wait_sent(phase)


def body(axes, mask_field, resist_goal, kernels, colour, active):
    core = mask_field.shape[0]
    tile = core + 2 * HALO
    kerns = kernels.shape[0]
    tables = make_tables(core, tile)
    f32, bf16 = jnp.float32, jnp.bfloat16
    vmem = pl.BlockSpec(memory_space=pltpu.VMEM)
    smem = pl.BlockSpec(memory_space=pltpu.SMEM)
    return pl.pallas_call(
        functools.partial(kernel, axes),
        out_shape=(
            jax.ShapeDtypeStruct((core, core), f32),
            jax.ShapeDtypeStruct((tile, tile), f32),
        ),
        in_specs=[vmem, vmem, vmem, smem, smem] + [vmem] * len(tables),
        out_specs=(vmem, vmem),
        scratch_shapes=[
            pltpu.VMEM((core, core), bf16),
            pltpu.VMEM((2, HALO, core), bf16),
            pltpu.VMEM((2, tile, 128), bf16),
            pltpu.VMEM((2, HALO, core), f32),
            pltpu.VMEM((2, tile, 128), f32),
            pltpu.VMEM((tile, tile), f32),
            pltpu.VMEM((tile, tile), bf16),
            pltpu.VMEM((ITERS, 9, FREQS + 16, 128), bf16),
            pltpu.VMEM((384, 384), bf16),
            pltpu.VMEM((kerns, FREQS, 128), f32),
            pltpu.VMEM((kerns, FREQS, 128), f32),
            pltpu.VMEM((core, core), f32),
            pltpu.VMEM((384, kerns * 256), bf16),
            pltpu.VMEM((core, kerns * 256), bf16),
            pltpu.VMEM((core, kerns * 256), bf16),
            pltpu.SemaphoreType.DMA((2 + ITERS, 9)),
            pltpu.SemaphoreType.DMA((2 + ITERS, 9)),
        ],
        compiler_params=pltpu.CompilerParams(
            collective_id=0, has_side_effects=True, vmem_limit_bytes=48 * 1024 * 1024
        ),
    )(
        mask_field,
        resist_goal,
        kernels.reshape(kerns, 2 * FREQS, FREQS),
        colour,
        active,
        *[jnp.asarray(table) for table in tables.values()],
    )


def solution(mesh):
    axes = mesh.axis_names
    return jax.shard_map(
        functools.partial(body, axes),
        mesh=mesh,
        in_specs=(P(*axes), P(*axes), P(), P(*axes), P(*axes)),
        out_specs=(P(*axes), P(*axes)),
        check_vma=False,
    )
```

```python
import functools
import math

import jax
import jax.numpy as jnp
import numpy as np
from jax import lax
from jax.experimental import pallas as pl
from jax.experimental.pallas import tpu as pltpu
from jax.sharding import PartitionSpec as P

HALO = 64
FREQS = 64
ITERS = 2
STEP_SIZE = 0.05
STEEPNESS = 4.0
THRESHOLD = 1.0
YBLOCK = 64

DIRS = [(di, dj) for di in (0, 1, -1) for dj in (0, 1, -1) if (di, dj) != (0, 0)]


def slot(di, dj):
    return 3 * (di % 3) + dj % 3


def make_tables(core, tile):
    bf16 = jnp.bfloat16
    place = (np.arange(tile) + HALO) % tile
    frequency = np.arange(FREQS) - FREQS // 2

    def waves(position):
        angle = (frequency[None, :] * position[:, None] % tile) * (2.0 * math.pi / tile)
        return np.concatenate([np.cos(angle), np.sin(angle)], 1)

    whole = waves(place).astype(np.float32)

    def split(table):
        table = table.astype(np.float32)
        high = table.astype(bf16)
        return high, (table - high.astype(np.float32)).astype(bf16)

    below = waves(place - core) * (place >= core)[:, None]
    above = waves(place + core) * (place < 2 * HALO)[:, None]
    spread = np.concatenate([whole, below, above], 1).astype(np.float32)
    samples = np.arange(2 * FREQS) * (tile // (2 * FREQS))
    wave_high, wave_low = split(waves(samples))
    apart = place[:core, None] - samples[None, :]
    difference = np.arange(1, FREQS)
    turns = difference[:, None, None] * apart[None] % tile * (2.0 * math.pi / tile)
    interpolate = (1.0 + 2.0 * np.cos(turns).sum(0)) / (2 * FREQS)
    fine_high, fine_low = split(interpolate)
    return dict(
        forward=np.ascontiguousarray((whole / tile).T).astype(bf16),
        whole=whole,
        half=np.concatenate([wave_high, wave_low, wave_high], 1),
        inverse_t=np.concatenate([wave_high.T, wave_high.T, wave_low.T], 0),
        inverse=np.concatenate([wave_high, wave_high], 0),
        half_t=np.concatenate([wave_high.T, wave_low.T], 1),
        fine=np.concatenate([fine_high, fine_low, fine_high], 1),
        fine_t=np.concatenate([fine_high.T, fine_high.T, fine_low.T], 0),
        rows=spread.astype(bf16),
        cols=np.ascontiguousarray((spread / tile).T).astype(bf16),
    )


def halves(value):
    high = value.astype(jnp.bfloat16)
    return high, (value - high.astype(jnp.float32)).astype(jnp.bfloat16)


def kernel(axes, count, colour_ref, active_ref, *refs):
    sources, (final_ref, next_ref) = refs[:count], refs[count : count + 2]
    held = refs[count + 2 : 2 * count + 2]
    run(axes, colour_ref, active_ref, sources, held, final_ref, next_ref, *refs[2 * count + 2 :])


def run(
    axes,
    colour_ref,
    active_ref,
    sources,
    held,
    final_ref,
    next_ref,
    mask16,
    vert16,
    side16,
    vert32,
    side32,
    window,
    image,
    grads,
    blocks,
    ka,
    kc,
    goal_t,
    weights,
    d_half,
    intensity,
    d_intensity,
    send_sems,
    recv_sems,
    load_sems,
):
    loads = [
        pltpu.make_async_copy(source, target, load_sems.at[at])
        for at, (source, target) in enumerate(zip(sources, held))
    ]
    for load in loads:
        load.start()
    mask_ref, goal_ref, kern_ref, forward_ref, whole_ref, half_ref = held[:6]
    inverse_t_ref, inverse_ref, half_t_ref, fine_ref, fine_t_ref, rows_ref, cols_ref = held[6:]
    core = mask_ref.shape[0]
    tile = core + 2 * HALO
    kerns = ka.shape[0]
    f32, bf16 = jnp.float32, jnp.bfloat16
    n_row, n_col = lax.axis_size(axes[0]), lax.axis_size(axes[1])
    row, col = lax.axis_index(axes[0]), lax.axis_index(axes[1])

    def exists(di, dj):
        there = (row + di >= 0) & (row + di < n_row)
        return there & (col + dj >= 0) & (col + dj < n_col)

    barrier = pltpu.get_barrier_semaphore()
    for di, dj in DIRS:

        @pl.when(exists(di, dj))
        def _(di=di, dj=dj):
            pl.semaphore_signal(
                barrier, inc=1, device_id=(row + di, col + dj), device_id_type=pl.DeviceIdType.MESH
            )

    def halo_refs(di, dj, source, vert, side):
        rows = {0: pl.ds(0, core), 1: pl.ds(core - HALO, HALO), -1: pl.ds(0, HALO)}[di]
        if dj == 0:
            return source.at[rows, :], vert.at[1 if di == 1 else 0]
        cols = pl.ds(core - 128, 128) if dj == 1 else pl.ds(0, 128)
        land = {0: pl.ds(0, core), 1: pl.ds(core + HALO, HALO), -1: pl.ds(core, HALO)}[di]
        return source.at[rows, cols], side.at[1 if dj == 1 else 0, land, :]

    def message(phase, di, dj, target):
        if phase < 2:
            pair = (mask16, vert16, side16) if phase == 0 else (mask_ref, vert32, side32)
            source, land = halo_refs(di, dj, *pair)
        else:
            source, land = grads.at[phase - 2, 0], grads.at[phase - 2, slot(-di, -dj)]
        return pltpu.make_async_remote_copy(
            src_ref=source,
            dst_ref=land,
            send_sem=send_sems.at[phase, slot(di, dj)],
            recv_sem=recv_sems.at[phase, slot(di, dj)],
            device_id=target,
            device_id_type=pl.DeviceIdType.MESH,
        )

    def send(phase):
        for di, dj in DIRS:

            @pl.when(exists(di, dj))
            def _(di=di, dj=dj):
                message(phase, di, dj, (row + di, col + dj)).start()

    def wait_arrivals(phase):
        for di, dj in DIRS:

            @pl.when(exists(-di, -dj))
            def _(di=di, dj=dj):
                message(phase, di, dj, (row - di, col - dj)).wait_recv()

    def wait_sent(phase):
        for di, dj in DIRS:

            @pl.when(exists(di, dj))
            def _(di=di, dj=dj):
                message(phase, di, dj, (row + di, col + dj)).wait_send()

    loads[0].wait()
    mask16[...] = mask_ref[...].astype(bf16)
    for di, dj in DIRS:

        @pl.when(jnp.logical_not(exists(di, dj)))
        def _(di=di, dj=dj):
            for vert, side in ((vert16, side16), (vert32, side32)):
                _, land = halo_refs(-di, -dj, mask_ref, vert, side)
                land[...] = jnp.zeros(land.shape, land.dtype)
            for step in range(ITERS):
                spot = grads.at[step, slot(di, dj)]
                spot[...] = jnp.zeros(spot.shape, spot.dtype)

    peers = sum(exists(di, dj).astype(jnp.int32) for di, dj in DIRS)
    pl.semaphore_wait(barrier, peers)

    send(0)
    send(1)

    for load in loads[1:]:
        load.wait()
    goal_t[...] = goal_ref[...].T
    for k in range(kerns):
        real, imag = kern_ref[k, :FREQS, :], kern_ref[k, FREQS:, :]
        ka[k] = jnp.concatenate([real, -imag], 0).T
        kc[k] = jnp.concatenate([imag, real], 0).T
    update = jnp.where(colour_ref[0, 0] == 0, 1.0, 0.0).astype(f32)
    active = active_ref[0, 0].astype(f32)
    left_half = lax.broadcasted_iota(jnp.int32, (1, 128), 1) < FREQS
    for step in range(ITERS):
        grads[step, 0, FREQS:, :] = jnp.full((16, 128), update, f32).astype(bf16)

    image[:core, :core] = mask16[...]
    window[:core, :core] = mask_ref[...]

    for step in range(ITERS):
        if step == 0:
            wait_arrivals(0)
            image[core : core + HALO, :core] = vert16[0]
            image[core + HALO :, :core] = vert16[1]
            image[:, core:] = jnp.where(
                left_half, side16[0].astype(f32), side16[1].astype(f32)
            ).astype(bf16)
        else:
            image[...] = window[...].astype(bf16)

        partial = lax.dot_general(
            forward_ref[...], image[...], (((1,), (1,)), ((), ())), preferred_element_type=f32
        )
        quads = jnp.dot(
            partial, whole_ref[...], precision=lax.Precision.HIGHEST, preferred_element_type=f32
        ) * (1.0 / tile)
        upper, lower = quads[:FREQS], quads[FREQS:]
        real = upper - pltpu.roll(lower, FREQS, 1)
        imag = -(lower + pltpu.roll(upper, FREQS, 1))
        real = jnp.where(left_half, real, pltpu.roll(real, FREQS, 1))
        imag = jnp.where(left_half, imag, pltpu.roll(imag, FREQS, 1))

        for k in range(kerns):
            x = ka[k] * real - kc[k] * imag
            y = kc[k] * real + ka[k] * imag
            both = jnp.concatenate([jnp.concatenate([x, -y], 0), jnp.concatenate([y, x], 0)], 1)
            high = both.astype(bf16)
            at = pl.ds(k * 256, 256)
            weights[:128, at] = high
            weights[128:256, at] = high
            weights[256:, at] = (both - high.astype(f32)).astype(bf16)
        halfway = jnp.dot(half_ref[...], weights[...], preferred_element_type=f32)
        high, low = halves(halfway)
        pieces = [slice(kp * 128, (kp + 1) * 128) for kp in range(2 * kerns)]
        high = jnp.concatenate([high[:, at] for at in pieces], 0)
        low = jnp.concatenate([low[:, at] for at in pieces], 0)
        fields = jnp.dot(
            jnp.concatenate([high, low, high], 1), inverse_t_ref[...], preferred_element_type=f32
        ).reshape(2 * kerns, 2 * FREQS, 2 * FREQS)
        high, low = halves(jnp.sum(fields * fields, axis=0))
        across = jnp.dot(
            jnp.concatenate([high, low, high], 1), fine_t_ref[...], preferred_element_type=f32
        )
        high, low = halves(across)
        intensity[...] = jnp.dot(
            fine_ref[...], jnp.concatenate([high, high, low], 0), preferred_element_type=f32
        )
        for start in range(0, core, YBLOCK):
            at = slice(start, start + YBLOCK)
            resist = 1.0 / (1.0 + jnp.exp(-STEEPNESS * (intensity[at, :] - THRESHOLD)))
            slope = (4.0 * STEEPNESS) * (resist - goal_t[at, :]) * (resist * (1.0 - resist))
            d_intensity[at, :] = slope.astype(bf16)
        d_across = jnp.dot(
            fine_t_ref[: 2 * FREQS, :], d_intensity[...], preferred_element_type=f32
        ).astype(bf16)
        d_samples = jnp.dot(d_across, fine_ref[:, : 2 * FREQS], preferred_element_type=f32)
        high, low = halves((fields * d_samples[None]).reshape(-1, 2 * FREQS))
        back = jnp.dot(
            jnp.concatenate([high, low], 1), inverse_ref[...], preferred_element_type=f32
        ).astype(bf16)
        for kp, at in enumerate(pieces):
            piece = back[kp * 128 : (kp + 1) * 128]
            d_half[:128, at] = piece
            d_half[128:, at] = piece

        d_weights = jnp.dot(half_t_ref[...], d_half[...], preferred_element_type=f32)
        d_real = jnp.zeros((FREQS, 128), f32)
        d_imag = jnp.zeros((FREQS, 128), f32)
        for k in range(kerns):
            at = k * 256
            dx = d_weights[:FREQS, at : at + 128] + d_weights[FREQS:, at + 128 : at + 256]
            dy = d_weights[:FREQS, at + 128 : at + 256] - d_weights[FREQS:, at : at + 128]
            d_real += ka[k] * dx + kc[k] * dy
            d_imag += ka[k] * dy - kc[k] * dx
        d_real = d_real + pltpu.roll(d_real, FREQS, 1)
        d_imag = d_imag + pltpu.roll(d_imag, FREQS, 1)
        own = jnp.where(left_half, d_real, -d_imag) * (active * (1.0 / tile))
        grads[step, 0, :FREQS, :] = own.astype(bf16)
        send(2 + step)
        if step == 0:
            wait_arrivals(1)
            window[core : core + HALO, :core] = vert32[0]
            window[core + HALO :, :core] = vert32[1]
            window[:, core:] = jnp.where(left_half, side32[0], side32[1])
        wait_arrivals(2 + step)

        for gi in range(3):
            for gj in range(3):
                top = grads[step, 3 * gi + gj, :FREQS, :].astype(f32)
                turned = pltpu.roll(top, FREQS, 1)
                low = jnp.where(left_half, turned, -turned)
                blocks[gj * 128 : gj * 128 + 128, gi * 128 : gi * 128 + 128] = jnp.concatenate(
                    [top, low], 0
                ).astype(bf16)
        spread = lax.dot_general(
            rows_ref[...], blocks[...], (((1,), (1,)), ((), ())), preferred_element_type=f32
        ).astype(bf16)
        total = jnp.dot(spread, cols_ref[...], preferred_element_type=f32)

        bands = ((0, core), (core, HALO), (core + HALO, HALO))
        for gi, (start, size) in enumerate(bands):
            flags = [grads[step, 3 * gi + gj, FREQS : FREQS + 16, :].astype(f32)[:1] for gj in range(3)]
            scale = jnp.concatenate(
                [flags[0]] * (core // 128) + [jnp.where(left_half, flags[1], flags[2])], 1
            )
            at = slice(start, start + size)
            fresh = jnp.clip(window[at, :] - STEP_SIZE * scale * total[at], -1.0, 1.0)
            if step < ITERS - 1:
                window[at, :] = fresh
            else:
                if gi == 0:
                    final_ref[...] = fresh[:, :core]
                out = (start + HALO) % tile
                next_ref[out : out + size, :] = pltpu.roll(fresh, HALO, 1)

    for phase in range(2 + ITERS):
        wait_sent(phase)


def body(axes, mask_field, resist_goal, kernels, colour, active):
    core = mask_field.shape[0]
    tile = core + 2 * HALO
    kerns = kernels.shape[0]
    tables = make_tables(core, tile)
    f32, bf16 = jnp.float32, jnp.bfloat16
    sources = [mask_field, resist_goal, kernels.reshape(kerns, 2 * FREQS, FREQS)]
    sources += [jnp.asarray(table) for table in tables.values()]
    vmem = pl.BlockSpec(memory_space=pltpu.VMEM)
    smem = pl.BlockSpec(memory_space=pltpu.SMEM)
    return pl.pallas_call(
        functools.partial(kernel, axes, len(sources)),
        out_shape=(
            jax.ShapeDtypeStruct((core, core), f32),
            jax.ShapeDtypeStruct((tile, tile), f32),
        ),
        in_specs=[smem, smem] + [pl.BlockSpec(memory_space=pltpu.HBM)] * len(sources),
        out_specs=(vmem, vmem),
        scratch_shapes=[pltpu.VMEM(source.shape, source.dtype) for source in sources]
        + [
            pltpu.VMEM((core, core), bf16),
            pltpu.VMEM((2, HALO, core), bf16),
            pltpu.VMEM((2, tile, 128), bf16),
            pltpu.VMEM((2, HALO, core), f32),
            pltpu.VMEM((2, tile, 128), f32),
            pltpu.VMEM((tile, tile), f32),
            pltpu.VMEM((tile, tile), bf16),
            pltpu.VMEM((ITERS, 9, FREQS + 16, 128), bf16),
            pltpu.VMEM((384, 384), bf16),
            pltpu.VMEM((kerns, FREQS, 128), f32),
            pltpu.VMEM((kerns, FREQS, 128), f32),
            pltpu.VMEM((core, core), f32),
            pltpu.VMEM((384, kerns * 256), bf16),
            pltpu.VMEM((256, kerns * 256), bf16),
            pltpu.VMEM((core, core), f32),
            pltpu.VMEM((core, core), bf16),
            pltpu.SemaphoreType.DMA((2 + ITERS, 9)),
            pltpu.SemaphoreType.DMA((2 + ITERS, 9)),
            pltpu.SemaphoreType.DMA((len(sources),)),
        ],
        compiler_params=pltpu.CompilerParams(
            collective_id=0, has_side_effects=True, vmem_limit_bytes=56 * 1024 * 1024
        ),
    )(
        colour,
        active,
        *sources,
    )


def solution(mesh):
    axes = mesh.axis_names
    return jax.shard_map(
        functools.partial(body, axes),
        mesh=mesh,
        in_specs=(P(*axes), P(*axes), P(), P(*axes), P(*axes)),
        out_specs=(P(*axes), P(*axes)),
        check_vma=False,
    )
```

```python
import functools
import math

import jax
import jax.numpy as jnp
import numpy as np
from jax import lax
from jax.experimental import pallas as pl
from jax.experimental.pallas import tpu as pltpu
from jax.sharding import PartitionSpec as P

HALO = 64
FREQS = 64
ITERS = 2
STEP_SIZE = 0.05
STEEPNESS = 4.0
THRESHOLD = 1.0
YBLOCK = 64

DIRS = [(1, 1), (-1, -1), (1, -1), (-1, 1), (1, 0), (-1, 0), (0, 1), (0, -1)]


def slot(di, dj):
    return 3 * (di % 3) + dj % 3


def make_tables(core, tile):
    bf16 = jnp.bfloat16
    place = (np.arange(tile) + HALO) % tile
    frequency = np.arange(FREQS) - FREQS // 2

    def waves(position):
        angle = (frequency[None, :] * position[:, None] % tile) * (2.0 * math.pi / tile)
        return np.concatenate([np.cos(angle), np.sin(angle)], 1)

    whole = waves(place).astype(np.float32)

    def split(table):
        table = table.astype(np.float32)
        high = table.astype(bf16)
        return high, (table - high.astype(np.float32)).astype(bf16)

    below = waves(place - core) * (place >= core)[:, None]
    above = waves(place + core) * (place < 2 * HALO)[:, None]
    spread = np.concatenate([whole, below, above], 1).astype(np.float32)
    samples = np.arange(2 * FREQS) * (tile // (2 * FREQS))
    wave_high, wave_low = split(waves(samples))
    apart = place[:core, None] - samples[None, :]
    difference = np.arange(1, FREQS)
    turns = difference[:, None, None] * apart[None] % tile * (2.0 * math.pi / tile)
    interpolate = (1.0 + 2.0 * np.cos(turns).sum(0)) / (2 * FREQS)
    fine_high, fine_low = split(interpolate)
    return dict(
        forward=np.ascontiguousarray((whole / tile).T).astype(bf16),
        whole=np.concatenate(split(whole)[:1] * 2 + split(whole)[1:], 0),
        half=np.concatenate([wave_high, wave_low, wave_high], 1),
        inverse_t=np.concatenate([wave_high.T, wave_high.T, wave_low.T], 0),
        inverse=np.concatenate([wave_high, wave_high], 0),
        half_t=np.concatenate([wave_high.T, wave_low.T], 1),
        fine=np.concatenate([fine_high, fine_low, fine_high], 1),
        fine_t=np.concatenate([fine_high.T, fine_high.T, fine_low.T], 0),
        rows=spread.astype(bf16),
        cols=np.ascontiguousarray((spread / tile).T).astype(bf16),
    )


def halves(value):
    high = value.astype(jnp.bfloat16)
    return high, (value - high.astype(jnp.float32)).astype(jnp.bfloat16)


def bands(core):
    return ((0, core), (core, HALO), (core + HALO, HALO))


def left_lanes():
    return lax.broadcasted_iota(jnp.int32, (1, 128), 1) < FREQS


def band_gradient(slots, blocks, rows_ref, cols_ref):
    f32, bf16 = jnp.float32, jnp.bfloat16
    for gi in range(3):
        for gj in range(3):
            top = slots[3 * gi + gj, :FREQS, :].astype(f32)
            turned = pltpu.roll(top, FREQS, 1)
            low = jnp.where(left_lanes(), turned, -turned)
            blocks[gj * 128 : gj * 128 + 128, gi * 128 : gi * 128 + 128] = jnp.concatenate(
                [top, low], 0
            ).astype(bf16)
    spread = lax.dot_general(
        rows_ref[...], blocks[...], (((1,), (1,)), ((), ())), preferred_element_type=f32
    ).astype(bf16)
    return jnp.dot(spread, cols_ref[...], preferred_element_type=f32)


def flag_row(slots, gi, core):
    flags = [slots[3 * gi + gj, FREQS : FREQS + 16, :].astype(jnp.float32)[:1] for gj in range(3)]
    sides = jnp.where(left_lanes(), flags[1], flags[2])
    return jnp.concatenate([flags[0]] * (core // 128) + [sides], 1)


def finish(
    last_ref, rows_src, cols_src, window_ref, final_ref, next_ref,
    last, rows, cols, window, blocks, final, following, load_sems, store_sems,
):
    loads = [
        pltpu.make_async_copy(source, target, load_sems.at[at])
        for at, (source, target) in enumerate(
            ((last_ref, last), (rows_src, rows), (cols_src, cols), (window_ref, window))
        )
    ]
    for load in loads:
        load.start()
    for load in loads:
        load.wait()
    core, tile = final.shape[0], following.shape[0]
    total = band_gradient(last, blocks, rows, cols)
    stores = []
    for gi, (start, size) in enumerate(bands(core)):
        at = slice(start, start + size)
        scale = flag_row(last, gi, core)
        fresh = jnp.clip(window[at, :] - STEP_SIZE * scale * total[at], -1.0, 1.0)
        out = pl.ds((start + HALO) % tile, size)
        following[out, :] = pltpu.roll(fresh, HALO, 1)
        stores.append(
            pltpu.make_async_copy(following.at[out, :], next_ref.at[out, :], store_sems.at[gi])
        )
        stores[-1].start()
        if gi == 0:
            final[...] = fresh[:, :core]
            stores.append(pltpu.make_async_copy(final, final_ref, store_sems.at[3]))
            stores[-1].start()
    for store in stores:
        store.wait()


def kernel(axes, count, colour_ref, active_ref, *refs):
    sources, (window_ref, last_ref) = refs[:count], refs[count : count + 2]
    held = refs[count + 2 : 2 * count + 2]
    run(axes, colour_ref, active_ref, sources, held, window_ref, last_ref, *refs[2 * count + 2 :])


def run(
    axes,
    colour_ref,
    active_ref,
    sources,
    held,
    window_ref,
    last_ref,
    mask16,
    vert16,
    side16,
    vert32,
    side32,
    window,
    image,
    grads,
    blocks,
    ka,
    kc,
    goal_t,
    weights,
    d_half,
    intensity,
    d_intensity,
    send_sems,
    recv_sems,
    load_sems,
    keep_sems,
):
    loads = [
        pltpu.make_async_copy(source, target, load_sems.at[at])
        for at, (source, target) in enumerate(zip(sources, held))
    ]
    for load in loads:
        load.start()
    mask_ref, goal_ref, kern_ref, forward_ref, whole_ref, half_ref = held[:6]
    inverse_t_ref, inverse_ref, half_t_ref, fine_ref, fine_t_ref, rows_ref, cols_ref = held[6:]
    core = mask_ref.shape[0]
    tile = core + 2 * HALO
    kerns = ka.shape[0]
    f32, bf16 = jnp.float32, jnp.bfloat16
    n_row, n_col = lax.axis_size(axes[0]), lax.axis_size(axes[1])
    row, col = lax.axis_index(axes[0]), lax.axis_index(axes[1])

    def exists(di, dj):
        there = (row + di >= 0) & (row + di < n_row)
        return there & (col + dj >= 0) & (col + dj < n_col)

    barrier = pltpu.get_barrier_semaphore()
    for di, dj in DIRS:

        @pl.when(exists(di, dj))
        def _(di=di, dj=dj):
            pl.semaphore_signal(
                barrier, inc=1, device_id=(row + di, col + dj), device_id_type=pl.DeviceIdType.MESH
            )

    def halo_refs(di, dj, source, vert, side):
        rows = {0: pl.ds(0, core), 1: pl.ds(core - HALO, HALO), -1: pl.ds(0, HALO)}[di]
        if dj == 0:
            return source.at[rows, :], vert.at[1 if di == 1 else 0]
        cols = pl.ds(core - 128, 128) if dj == 1 else pl.ds(0, 128)
        land = {0: pl.ds(0, core), 1: pl.ds(core + HALO, HALO), -1: pl.ds(core, HALO)}[di]
        return source.at[rows, cols], side.at[1 if dj == 1 else 0, land, :]

    def slots_of(step):
        return last_ref if step == ITERS - 1 else grads.at[step]

    def blank(di, dj):
        at = slot(di, dj)
        return pltpu.make_async_copy(grads.at[ITERS - 1, at], last_ref.at[at], keep_sems.at[at])

    keep_own = pltpu.make_async_copy(grads.at[ITERS - 1, 0], last_ref.at[0], keep_sems.at[0])
    keep_window = pltpu.make_async_copy(window, window_ref, keep_sems.at[9])

    def message(phase, di, dj, target):
        if phase < 2:
            pair = (mask16, vert16, side16) if phase == 0 else (mask_ref, vert32, side32)
            source, land = halo_refs(di, dj, *pair)
        else:
            source, land = grads.at[phase - 2, 0], slots_of(phase - 2).at[slot(-di, -dj)]
        return pltpu.make_async_remote_copy(
            src_ref=source,
            dst_ref=land,
            send_sem=send_sems.at[phase, slot(di, dj)],
            recv_sem=recv_sems.at[phase, slot(di, dj)],
            device_id=target,
            device_id_type=pl.DeviceIdType.MESH,
        )

    def send(phase):
        for di, dj in DIRS:

            @pl.when(exists(di, dj))
            def _(di=di, dj=dj):
                message(phase, di, dj, (row + di, col + dj)).start()

    def wait_arrivals(phase):
        for di, dj in DIRS:

            @pl.when(exists(-di, -dj))
            def _(di=di, dj=dj):
                message(phase, di, dj, (row - di, col - dj)).wait_recv()

    def wait_sent(phase):
        for di, dj in DIRS:

            @pl.when(exists(di, dj))
            def _(di=di, dj=dj):
                message(phase, di, dj, (row + di, col + dj)).wait_send()

    loads[0].wait()
    mask16[...] = mask_ref[...].astype(bf16)
    for di, dj in DIRS:

        @pl.when(jnp.logical_not(exists(di, dj)))
        def _(di=di, dj=dj):
            for vert, side in ((vert16, side16), (vert32, side32)):
                _, land = halo_refs(-di, -dj, mask_ref, vert, side)
                land[...] = jnp.zeros(land.shape, land.dtype)
            for step in range(ITERS):
                spot = grads.at[step, slot(di, dj)]
                spot[...] = jnp.zeros(spot.shape, spot.dtype)
            blank(di, dj).start()

    peers = sum(exists(di, dj).astype(jnp.int32) for di, dj in DIRS)
    pl.semaphore_wait(barrier, peers)

    send(0)

    for load in loads[1:]:
        load.wait()
    goal_t[...] = goal_ref[...].T
    for k in range(kerns):
        real, imag = kern_ref[k, :FREQS, :], kern_ref[k, FREQS:, :]
        ka[k] = jnp.concatenate([real, -imag], 0).T
        kc[k] = jnp.concatenate([imag, real], 0).T
    update = jnp.where(colour_ref[0, 0] == 0, 1.0, 0.0).astype(f32)
    active = active_ref[0, 0].astype(f32)
    left_half = lax.broadcasted_iota(jnp.int32, (1, 128), 1) < FREQS
    for step in range(ITERS):
        grads[step, 0, FREQS:, :] = jnp.full((16, 128), update, f32).astype(bf16)

    image[:core, :core] = mask16[...]
    window[:core, :core] = mask_ref[...]

    for step in range(ITERS):
        if step == 0:
            wait_arrivals(0)
            send(1)
            image[core : core + HALO, :core] = vert16[0]
            image[core + HALO :, :core] = vert16[1]
            image[:, core:] = jnp.where(
                left_half, side16[0].astype(f32), side16[1].astype(f32)
            ).astype(bf16)
        else:
            image[...] = window[...].astype(bf16)

        partial = lax.dot_general(
            forward_ref[...], image[...], (((1,), (1,)), ((), ())), preferred_element_type=f32
        )
        high, low = halves(partial)
        quads = jnp.dot(
            jnp.concatenate([high, low, high], 1), whole_ref[...], preferred_element_type=f32
        ) * (1.0 / tile)
        upper, lower = quads[:FREQS], quads[FREQS:]
        real = upper - pltpu.roll(lower, FREQS, 1)
        imag = -(lower + pltpu.roll(upper, FREQS, 1))
        real = jnp.where(left_half, real, pltpu.roll(real, FREQS, 1))
        imag = jnp.where(left_half, imag, pltpu.roll(imag, FREQS, 1))

        for k in range(kerns):
            x = ka[k] * real - kc[k] * imag
            y = kc[k] * real + ka[k] * imag
            both = jnp.concatenate([jnp.concatenate([x, -y], 0), jnp.concatenate([y, x], 0)], 1)
            high = both.astype(bf16)
            at = pl.ds(k * 256, 256)
            weights[:128, at] = high
            weights[128:256, at] = high
            weights[256:, at] = (both - high.astype(f32)).astype(bf16)
        halfway = jnp.dot(half_ref[...], weights[...], preferred_element_type=f32)
        high, low = halves(halfway)
        pieces = [slice(kp * 128, (kp + 1) * 128) for kp in range(2 * kerns)]
        high = jnp.concatenate([high[:, at] for at in pieces], 0)
        low = jnp.concatenate([low[:, at] for at in pieces], 0)
        fields = jnp.dot(
            jnp.concatenate([high, low, high], 1), inverse_t_ref[...], preferred_element_type=f32
        ).reshape(2 * kerns, 2 * FREQS, 2 * FREQS)
        high, low = halves(jnp.sum(fields * fields, axis=0))
        across = jnp.dot(
            jnp.concatenate([high, low, high], 1), fine_t_ref[...], preferred_element_type=f32
        )
        high, low = halves(across)
        intensity[...] = jnp.dot(
            fine_ref[...], jnp.concatenate([high, high, low], 0), preferred_element_type=f32
        )
        for start in range(0, core, YBLOCK):
            at = slice(start, start + YBLOCK)
            resist = 1.0 / (1.0 + jnp.exp(-STEEPNESS * (intensity[at, :] - THRESHOLD)))
            slope = (4.0 * STEEPNESS) * (resist - goal_t[at, :]) * (resist * (1.0 - resist))
            d_intensity[at, :] = slope.astype(bf16)
        d_across = jnp.dot(
            fine_t_ref[: 2 * FREQS, :], d_intensity[...], preferred_element_type=f32
        ).astype(bf16)
        d_samples = jnp.dot(d_across, fine_ref[:, : 2 * FREQS], preferred_element_type=f32)
        high, low = halves((fields * d_samples[None]).reshape(-1, 2 * FREQS))
        back = jnp.dot(
            jnp.concatenate([high, low], 1), inverse_ref[...], preferred_element_type=f32
        ).astype(bf16)
        for kp, at in enumerate(pieces):
            piece = back[kp * 128 : (kp + 1) * 128]
            d_half[:128, at] = piece
            d_half[128:, at] = piece

        d_weights = jnp.dot(half_t_ref[...], d_half[...], preferred_element_type=f32)
        d_real = jnp.zeros((FREQS, 128), f32)
        d_imag = jnp.zeros((FREQS, 128), f32)
        for k in range(kerns):
            at = k * 256
            dx = d_weights[:FREQS, at : at + 128] + d_weights[FREQS:, at + 128 : at + 256]
            dy = d_weights[:FREQS, at + 128 : at + 256] - d_weights[FREQS:, at : at + 128]
            d_real += ka[k] * dx + kc[k] * dy
            d_imag += ka[k] * dy - kc[k] * dx
        d_real = d_real + pltpu.roll(d_real, FREQS, 1)
        d_imag = d_imag + pltpu.roll(d_imag, FREQS, 1)
        own = jnp.where(left_half, d_real, -d_imag) * (active * (1.0 / tile))
        grads[step, 0, :FREQS, :] = own.astype(bf16)
        send(2 + step)
        if step == ITERS - 1:
            keep_own.start()
            keep_window.start()
        if step == 0:
            wait_arrivals(1)
            window[core : core + HALO, :core] = vert32[0]
            window[core + HALO :, :core] = vert32[1]
            window[:, core:] = jnp.where(left_half, side32[0], side32[1])
        wait_arrivals(2 + step)

        if step < ITERS - 1:
            total = band_gradient(grads.at[step], blocks, rows_ref, cols_ref)
            for gi, (start, size) in enumerate(bands(core)):
                at = slice(start, start + size)
                scale = flag_row(grads.at[step], gi, core)
                window[at, :] = jnp.clip(window[at, :] - STEP_SIZE * scale * total[at], -1.0, 1.0)
    keep_window.wait()
    keep_own.wait()
    for di, dj in DIRS:

        @pl.when(jnp.logical_not(exists(di, dj)))
        def _(di=di, dj=dj):
            blank(di, dj).wait()

    for phase in range(2 + ITERS):
        wait_sent(phase)


def body(axes, mask_field, resist_goal, kernels, colour, active):
    core = mask_field.shape[0]
    tile = core + 2 * HALO
    kerns = kernels.shape[0]
    tables = make_tables(core, tile)
    f32, bf16 = jnp.float32, jnp.bfloat16
    sources = [mask_field, resist_goal, kernels.reshape(kerns, 2 * FREQS, FREQS)]
    sources += [jnp.asarray(table) for table in tables.values()]
    hbm = pl.BlockSpec(memory_space=pltpu.HBM)
    smem = pl.BlockSpec(memory_space=pltpu.SMEM)
    window, last = pl.pallas_call(
        functools.partial(kernel, axes, len(sources)),
        out_shape=(
            jax.ShapeDtypeStruct((tile, tile), f32),
            jax.ShapeDtypeStruct((9, FREQS + 16, 128), bf16),
        ),
        in_specs=[smem, smem] + [hbm] * len(sources),
        out_specs=(hbm, hbm),
        scratch_shapes=[pltpu.VMEM(source.shape, source.dtype) for source in sources]
        + [
            pltpu.VMEM((core, core), bf16),
            pltpu.VMEM((2, HALO, core), bf16),
            pltpu.VMEM((2, tile, 128), bf16),
            pltpu.VMEM((2, HALO, core), f32),
            pltpu.VMEM((2, tile, 128), f32),
            pltpu.VMEM((tile, tile), f32),
            pltpu.VMEM((tile, tile), bf16),
            pltpu.VMEM((ITERS, 9, FREQS + 16, 128), bf16),
            pltpu.VMEM((384, 384), bf16),
            pltpu.VMEM((kerns, FREQS, 128), f32),
            pltpu.VMEM((kerns, FREQS, 128), f32),
            pltpu.VMEM((core, core), f32),
            pltpu.VMEM((384, kerns * 256), bf16),
            pltpu.VMEM((256, kerns * 256), bf16),
            pltpu.VMEM((core, core), f32),
            pltpu.VMEM((core, core), bf16),
            pltpu.SemaphoreType.DMA((2 + ITERS, 9)),
            pltpu.SemaphoreType.DMA((2 + ITERS, 9)),
            pltpu.SemaphoreType.DMA((len(sources),)),
            pltpu.SemaphoreType.DMA((10,)),
        ],
        compiler_params=pltpu.CompilerParams(
            collective_id=0, has_side_effects=True, vmem_limit_bytes=56 * 1024 * 1024
        ),
    )(
        colour,
        active,
        *sources,
    )
    finals = [last, sources[-2], sources[-1], window]
    return pl.pallas_call(
        finish,
        out_shape=(
            jax.ShapeDtypeStruct((core, core), f32),
            jax.ShapeDtypeStruct((tile, tile), f32),
        ),
        in_specs=[hbm] * len(finals),
        out_specs=(hbm, hbm),
        scratch_shapes=[pltpu.VMEM(source.shape, source.dtype) for source in finals]
        + [
            pltpu.VMEM((384, 384), bf16),
            pltpu.VMEM((core, core), f32),
            pltpu.VMEM((tile, tile), f32),
            pltpu.SemaphoreType.DMA((4,)),
            pltpu.SemaphoreType.DMA((4,)),
        ],
        compiler_params=pltpu.CompilerParams(vmem_limit_bytes=56 * 1024 * 1024),
    )(*finals)


def solution(mesh):
    axes = mesh.axis_names
    return jax.shard_map(
        functools.partial(body, axes),
        mesh=mesh,
        in_specs=(P(*axes), P(*axes), P(), P(*axes), P(*axes)),
        out_specs=(P(*axes), P(*axes)),
        check_vma=False,
    )
```

```python
import functools
import math

import jax
import jax.numpy as jnp
import numpy as np
from jax import lax
from jax.experimental import pallas as pl
from jax.experimental.pallas import tpu as pltpu
from jax.sharding import PartitionSpec as P

HALO = 64
FREQS = 64
ITERS = 2
STEP_SIZE = 0.05
STEEPNESS = 4.0
THRESHOLD = 1.0
YBLOCK = 64
FLAG_LANE = FREQS + FREQS // 2

DIRS = [(1, 1), (-1, -1), (1, -1), (-1, 1), (1, 0), (-1, 0), (0, 1), (0, -1)]


def slot(di, dj):
    return 3 * (di % 3) + dj % 3


def make_tables(core, tile):
    bf16 = jnp.bfloat16
    place = (np.arange(tile) + HALO) % tile
    frequency = np.arange(FREQS) - FREQS // 2

    def waves(position):
        angle = (frequency[None, :] * position[:, None] % tile) * (2.0 * math.pi / tile)
        return np.concatenate([np.cos(angle), np.sin(angle)], 1)

    whole = waves(place).astype(np.float32)

    def split(table):
        table = table.astype(np.float32)
        high = table.astype(bf16)
        return high, (table - high.astype(np.float32)).astype(bf16)

    below = waves(place - core) * (place >= core)[:, None]
    above = waves(place + core) * (place < 2 * HALO)[:, None]
    spread = np.concatenate([whole, below, above], 1).astype(np.float32)
    samples = np.arange(2 * FREQS) * (tile // (2 * FREQS))
    wave_high, wave_low = split(waves(samples))
    apart = place[:core, None] - samples[None, :]
    difference = np.arange(1, FREQS)
    turns = difference[:, None, None] * apart[None] % tile * (2.0 * math.pi / tile)
    interpolate = (1.0 + 2.0 * np.cos(turns).sum(0)) / (2 * FREQS)
    fine_high, fine_low = split(interpolate)
    return dict(
        forward=np.ascontiguousarray((whole / tile).T).astype(bf16),
        whole=np.concatenate(split(whole)[:1] * 2 + split(whole)[1:], 0),
        half=np.concatenate([wave_high, wave_low], 1),
        inverse_t=np.concatenate([wave_high.T, wave_low.T], 0),
        inverse=wave_high,
        half_t=np.concatenate([wave_high.T, wave_low.T], 1),
        fine=np.concatenate([fine_high, fine_low, fine_high], 1),
        fine_t=np.concatenate([fine_high.T, fine_high.T, fine_low.T], 0),
        rows=spread.astype(bf16),
        cols=np.ascontiguousarray((spread / tile).T).astype(bf16),
    )


def halves(value):
    high = value.astype(jnp.bfloat16)
    return high, (value - high.astype(jnp.float32)).astype(jnp.bfloat16)


def whole_of(high, low):
    return high.astype(jnp.float32) + low.astype(jnp.float32)


def bands(core):
    return ((0, core), (core, HALO), (core + HALO, HALO))


def left_lanes():
    return lax.broadcasted_iota(jnp.int32, (1, 128), 1) < FREQS


def band_gradient(slots, blocks, rows_ref, cols_ref, loads=()):
    f32, bf16 = jnp.float32, jnp.bfloat16
    for gi in range(3):
        for gj in range(3):
            top = slots[3 * gi + gj].astype(f32)
            turned = pltpu.roll(top, FREQS, 1)
            low = jnp.where(left_lanes(), turned, -turned)
            blocks[gj * 128 : gj * 128 + 128, gi * 128 : gi * 128 + 128] = jnp.concatenate(
                [top, low], 0
            ).astype(bf16)
    for load in loads:
        load.wait()
    spread = lax.dot_general(
        rows_ref[...], blocks[...], (((1,), (1,)), ((), ())), preferred_element_type=f32
    ).astype(bf16)
    return jnp.dot(spread, cols_ref[...], preferred_element_type=f32)


def flag_row(slots, gi, core):
    at = FREQS // 2
    here = lax.broadcasted_iota(jnp.int32, (1, 128), 1) == FLAG_LANE
    flags = [slots[3 * gi + gj, at : at + 16, :].astype(jnp.float32)[:1] for gj in range(3)]
    flags = [jnp.sum(jnp.where(here, flag, 0.0), axis=1, keepdims=True) for flag in flags]
    flags = [jnp.broadcast_to(flag, (1, 128)) for flag in flags]
    sides = jnp.where(left_lanes(), flags[1], flags[2])
    return jnp.concatenate([flags[0]] * (core // 128) + [sides], 1)


def finish(
    last_ref, rows_src, cols_src, window_ref, final_ref, next_ref,
    last, rows, cols, window, blocks, final, following, load_sems, store_sems,
):
    loads = [
        pltpu.make_async_copy(source, target, load_sems.at[at])
        for at, (source, target) in enumerate(
            ((last_ref, last), (rows_src, rows), (cols_src, cols), (window_ref, window))
        )
    ]
    for load in loads:
        load.start()
    core, tile = final.shape[0], following.shape[0]
    loads[0].wait()
    total = band_gradient(last, blocks, rows, cols, loads[1:3])
    loads[3].wait()
    stores = []
    for gi, (start, size) in enumerate(bands(core)):
        at = slice(start, start + size)
        scale = flag_row(last, gi, core)
        fresh = jnp.clip(window[at, :] - STEP_SIZE * scale * total[at], -1.0, 1.0)
        out = pl.ds((start + HALO) % tile, size)
        following[out, :] = pltpu.roll(fresh, HALO, 1)
        stores.append(
            pltpu.make_async_copy(following.at[out, :], next_ref.at[out, :], store_sems.at[gi])
        )
        stores[-1].start()
        if gi == 0:
            final[...] = fresh[:, :core]
            stores.append(pltpu.make_async_copy(final, final_ref, store_sems.at[3]))
            stores[-1].start()
    for store in stores:
        store.wait()


def kernel(axes, count, colour_ref, active_ref, *refs):
    sources, (window_ref, last_ref) = refs[:count], refs[count : count + 2]
    held = refs[count + 2 : 2 * count + 2]
    run(axes, colour_ref, active_ref, sources, held, window_ref, last_ref, *refs[2 * count + 2 :])


def run(
    axes,
    colour_ref,
    active_ref,
    sources,
    held,
    window_ref,
    last_ref,
    mask16,
    rest16,
    vert16,
    side16,
    vert_rest,
    side_rest,
    window,
    image,
    grads,
    blocks,
    ka,
    kc,
    goal_t,
    weights,
    d_half,
    intensity,
    d_intensity,
    send_sems,
    recv_sems,
    load_sems,
    keep_sems,
):
    loads = [
        pltpu.make_async_copy(source, target, load_sems.at[at])
        for at, (source, target) in enumerate(zip(sources, held))
    ]
    loads[0].start()
    mask_ref, goal_ref, kern_ref, forward_ref, whole_ref, half_ref = held[:6]
    inverse_t_ref, inverse_ref, half_t_ref, fine_ref, fine_t_ref, rows_ref, cols_ref = held[6:]
    core = mask_ref.shape[0]
    tile = core + 2 * HALO
    kerns = ka.shape[0]
    f32, bf16 = jnp.float32, jnp.bfloat16
    n_row, n_col = lax.axis_size(axes[0]), lax.axis_size(axes[1])
    row, col = lax.axis_index(axes[0]), lax.axis_index(axes[1])

    def exists(di, dj):
        there = (row + di >= 0) & (row + di < n_row)
        return there & (col + dj >= 0) & (col + dj < n_col)

    barrier = pltpu.get_barrier_semaphore()
    for di, dj in DIRS:

        @pl.when(exists(di, dj))
        def _(di=di, dj=dj):
            pl.semaphore_signal(
                barrier, inc=1, device_id=(row + di, col + dj), device_id_type=pl.DeviceIdType.MESH
            )

    def halo_refs(di, dj, source, vert, side):
        rows = {0: pl.ds(0, core), 1: pl.ds(core - HALO, HALO), -1: pl.ds(0, HALO)}[di]
        if dj == 0:
            return source.at[rows, :], vert.at[1 if di == 1 else 0]
        cols = pl.ds(core - 128, 128) if dj == 1 else pl.ds(0, 128)
        land = {0: pl.ds(0, core), 1: pl.ds(core + HALO, HALO), -1: pl.ds(core, HALO)}[di]
        return source.at[rows, cols], side.at[1 if dj == 1 else 0, land, :]

    def slots_of(step):
        return last_ref if step == ITERS - 1 else grads.at[step]

    def blank(di, dj):
        at = slot(di, dj)
        return pltpu.make_async_copy(grads.at[ITERS - 1, at], last_ref.at[at], keep_sems.at[at])

    keep_own = pltpu.make_async_copy(grads.at[ITERS - 1, 0], last_ref.at[0], keep_sems.at[0])
    keep_window = pltpu.make_async_copy(window, window_ref, keep_sems.at[9])

    def message(phase, di, dj, target):
        if phase < 2:
            pair = (mask16, vert16, side16) if phase == 0 else (rest16, vert_rest, side_rest)
            source, land = halo_refs(di, dj, *pair)
        else:
            source, land = grads.at[phase - 2, 0], slots_of(phase - 2).at[slot(-di, -dj)]
        return pltpu.make_async_remote_copy(
            src_ref=source,
            dst_ref=land,
            send_sem=send_sems.at[phase, slot(di, dj)],
            recv_sem=recv_sems.at[phase, slot(di, dj)],
            device_id=target,
            device_id_type=pl.DeviceIdType.MESH,
        )

    def send(phase):
        for di, dj in DIRS:

            @pl.when(exists(di, dj))
            def _(di=di, dj=dj):
                message(phase, di, dj, (row + di, col + dj)).start()

    def wait_arrivals(phase):
        for di, dj in DIRS:

            @pl.when(exists(-di, -dj))
            def _(di=di, dj=dj):
                message(phase, di, dj, (row - di, col - dj)).wait_recv()

    def wait_sent(phase):
        for di, dj in DIRS:

            @pl.when(exists(di, dj))
            def _(di=di, dj=dj):
                message(phase, di, dj, (row + di, col + dj)).wait_send()

    loads[0].wait()
    for load in loads[1:]:
        load.start()
    mask16[...], rest16[...] = halves(mask_ref[...])
    for di, dj in DIRS:

        @pl.when(jnp.logical_not(exists(di, dj)))
        def _(di=di, dj=dj):
            for vert, side in ((vert16, side16), (vert_rest, side_rest)):
                _, land = halo_refs(-di, -dj, mask_ref, vert, side)
                land[...] = jnp.zeros(land.shape, land.dtype)
            for step in range(ITERS):
                spot = grads.at[step, slot(di, dj)]
                spot[...] = jnp.zeros(spot.shape, spot.dtype)
            blank(di, dj).start()

    peers = sum(exists(di, dj).astype(jnp.int32) for di, dj in DIRS)
    pl.semaphore_wait(barrier, peers)

    send(0)

    for load in loads[1:]:
        load.wait()
    goal_t[...] = goal_ref[...].T
    for k in range(kerns):
        real, imag = kern_ref[k, :FREQS, :], kern_ref[k, FREQS:, :]
        ka[k] = jnp.concatenate([real, -imag], 0).T
        kc[k] = jnp.concatenate([imag, real], 0).T
    update = jnp.where(colour_ref[0, 0] == 0, 1.0, 0.0).astype(f32)
    active = active_ref[0, 0].astype(f32)
    left_half = lax.broadcasted_iota(jnp.int32, (1, 128), 1) < FREQS
    flag_spot = lax.broadcasted_iota(jnp.int32, (FREQS, 128), 0) == FREQS // 2
    flag_spot &= lax.broadcasted_iota(jnp.int32, (FREQS, 128), 1) == FLAG_LANE

    image[:core, :core] = mask16[...]
    window[:core, :core] = mask_ref[...]

    for step in range(ITERS):
        if step == 0:
            wait_arrivals(0)
            send(1)
            image[core : core + HALO, :core] = vert16[0]
            image[core + HALO :, :core] = vert16[1]
            image[:, core:] = jnp.where(
                left_half, side16[0].astype(f32), side16[1].astype(f32)
            ).astype(bf16)
        else:
            image[...] = window[...].astype(bf16)

        partial = lax.dot_general(
            forward_ref[...], image[...], (((1,), (1,)), ((), ())), preferred_element_type=f32
        )
        high, low = halves(partial)
        quads = jnp.dot(
            jnp.concatenate([high, low, high], 1), whole_ref[...], preferred_element_type=f32
        ) * (1.0 / tile)
        upper, lower = quads[:FREQS], quads[FREQS:]
        real = upper - pltpu.roll(lower, FREQS, 1)
        imag = -(lower + pltpu.roll(upper, FREQS, 1))
        real = jnp.where(left_half, real, pltpu.roll(real, FREQS, 1))
        imag = jnp.where(left_half, imag, pltpu.roll(imag, FREQS, 1))

        for k in range(kerns):
            x = ka[k] * real - kc[k] * imag
            y = kc[k] * real + ka[k] * imag
            both = jnp.concatenate([jnp.concatenate([x, -y], 0), jnp.concatenate([y, x], 0)], 1)
            high = both.astype(bf16)
            at = pl.ds(k * 256, 256)
            weights[:128, at] = high
            weights[128:, at] = high
        halfway = jnp.dot(half_ref[...], weights[...], preferred_element_type=f32).astype(bf16)
        pieces = [slice(kp * 128, (kp + 1) * 128) for kp in range(2 * kerns)]
        stacked = jnp.concatenate([halfway[:, at] for at in pieces], 0)
        fields = jnp.dot(
            jnp.concatenate([stacked, stacked], 1), inverse_t_ref[...], preferred_element_type=f32
        ).reshape(2 * kerns, 2 * FREQS, 2 * FREQS)
        high, low = halves(jnp.sum(fields * fields, axis=0))
        across = jnp.dot(
            jnp.concatenate([high, low, high], 1), fine_t_ref[...], preferred_element_type=f32
        )
        high, low = halves(across)
        intensity[...] = jnp.dot(
            fine_ref[...], jnp.concatenate([high, high, low], 0), preferred_element_type=f32
        )
        for start in range(0, core, YBLOCK):
            at = slice(start, start + YBLOCK)
            resist = 1.0 / (1.0 + jnp.exp(-STEEPNESS * (intensity[at, :] - THRESHOLD)))
            slope = (4.0 * STEEPNESS) * (resist - goal_t[at, :]) * (resist * (1.0 - resist))
            d_intensity[at, :] = slope.astype(bf16)
        d_across = jnp.dot(
            fine_t_ref[: 2 * FREQS, :], d_intensity[...], preferred_element_type=f32
        ).astype(bf16)
        d_samples = jnp.dot(d_across, fine_ref[:, : 2 * FREQS], preferred_element_type=f32)
        d_fields = (fields * d_samples[None]).astype(bf16).reshape(-1, 2 * FREQS)
        back = jnp.dot(d_fields, inverse_ref[...], preferred_element_type=f32).astype(bf16)
        for kp, at in enumerate(pieces):
            piece = back[kp * 128 : (kp + 1) * 128]
            d_half[:128, at] = piece
            d_half[128:, at] = piece

        d_weights = jnp.dot(half_t_ref[...], d_half[...], preferred_element_type=f32)
        d_real = jnp.zeros((FREQS, 128), f32)
        d_imag = jnp.zeros((FREQS, 128), f32)
        for k in range(kerns):
            at = k * 256
            dx = d_weights[:FREQS, at : at + 128] + d_weights[FREQS:, at + 128 : at + 256]
            dy = d_weights[:FREQS, at + 128 : at + 256] - d_weights[FREQS:, at : at + 128]
            d_real += ka[k] * dx + kc[k] * dy
            d_imag += ka[k] * dy - kc[k] * dx
        d_real = d_real + pltpu.roll(d_real, FREQS, 1)
        d_imag = d_imag + pltpu.roll(d_imag, FREQS, 1)
        own = jnp.where(left_half, d_real, -d_imag) * (active * (1.0 / tile))
        grads[step, 0] = jnp.where(flag_spot, update, own).astype(bf16)
        send(2 + step)
        if step == ITERS - 1:
            keep_own.start()
            keep_window.start()
        if step == 0:
            wait_arrivals(1)
            for at in (0, 1):
                start = core + at * HALO
                window[start : start + HALO, :core] = whole_of(vert16[at], vert_rest[at])
            window[:, core:] = jnp.where(
                left_half, whole_of(side16[0], side_rest[0]), whole_of(side16[1], side_rest[1])
            )
        wait_arrivals(2 + step)

        if step < ITERS - 1:
            total = band_gradient(grads.at[step], blocks, rows_ref, cols_ref)
            for gi, (start, size) in enumerate(bands(core)):
                at = slice(start, start + size)
                scale = flag_row(grads.at[step], gi, core)
                window[at, :] = jnp.clip(window[at, :] - STEP_SIZE * scale * total[at], -1.0, 1.0)
    keep_window.wait()
    keep_own.wait()
    for di, dj in DIRS:

        @pl.when(jnp.logical_not(exists(di, dj)))
        def _(di=di, dj=dj):
            blank(di, dj).wait()

    for phase in range(2 + ITERS):
        wait_sent(phase)


def body(axes, mask_field, resist_goal, kernels, colour, active):
    core = mask_field.shape[0]
    tile = core + 2 * HALO
    kerns = kernels.shape[0]
    tables = make_tables(core, tile)
    f32, bf16 = jnp.float32, jnp.bfloat16
    sources = [mask_field, resist_goal, kernels.reshape(kerns, 2 * FREQS, FREQS)]
    sources += [jnp.asarray(table) for table in tables.values()]
    hbm = pl.BlockSpec(memory_space=pltpu.HBM)
    smem = pl.BlockSpec(memory_space=pltpu.SMEM)
    window, last = pl.pallas_call(
        functools.partial(kernel, axes, len(sources)),
        out_shape=(
            jax.ShapeDtypeStruct((tile, tile), f32),
            jax.ShapeDtypeStruct((9, FREQS, 128), bf16),
        ),
        in_specs=[smem, smem] + [hbm] * len(sources),
        out_specs=(hbm, hbm),
        scratch_shapes=[pltpu.VMEM(source.shape, source.dtype) for source in sources]
        + [
            pltpu.VMEM((core, core), bf16),
            pltpu.VMEM((core, core), bf16),
            pltpu.VMEM((2, HALO, core), bf16),
            pltpu.VMEM((2, tile, 128), bf16),
            pltpu.VMEM((2, HALO, core), bf16),
            pltpu.VMEM((2, tile, 128), bf16),
            pltpu.VMEM((tile, tile), f32),
            pltpu.VMEM((tile, tile), bf16),
            pltpu.VMEM((ITERS, 9, FREQS, 128), bf16),
            pltpu.VMEM((384, 384), bf16),
            pltpu.VMEM((kerns, FREQS, 128), f32),
            pltpu.VMEM((kerns, FREQS, 128), f32),
            pltpu.VMEM((core, core), f32),
            pltpu.VMEM((256, kerns * 256), bf16),
            pltpu.VMEM((256, kerns * 256), bf16),
            pltpu.VMEM((core, core), f32),
            pltpu.VMEM((core, core), bf16),
            pltpu.SemaphoreType.DMA((2 + ITERS, 9)),
            pltpu.SemaphoreType.DMA((2 + ITERS, 9)),
            pltpu.SemaphoreType.DMA((len(sources),)),
            pltpu.SemaphoreType.DMA((10,)),
        ],
        compiler_params=pltpu.CompilerParams(
            collective_id=0, has_side_effects=True, vmem_limit_bytes=56 * 1024 * 1024
        ),
    )(
        colour,
        active,
        *sources,
    )
    finals = [last, sources[-2], sources[-1], window]
    return pl.pallas_call(
        finish,
        out_shape=(
            jax.ShapeDtypeStruct((core, core), f32),
            jax.ShapeDtypeStruct((tile, tile), f32),
        ),
        in_specs=[hbm] * len(finals),
        out_specs=(hbm, hbm),
        scratch_shapes=[pltpu.VMEM(source.shape, source.dtype) for source in finals]
        + [
            pltpu.VMEM((384, 384), bf16),
            pltpu.VMEM((core, core), f32),
            pltpu.VMEM((tile, tile), f32),
            pltpu.SemaphoreType.DMA((4,)),
            pltpu.SemaphoreType.DMA((4,)),
        ],
        compiler_params=pltpu.CompilerParams(vmem_limit_bytes=56 * 1024 * 1024),
    )(*finals)


def solution(mesh):
    axes = mesh.axis_names
    return jax.shard_map(
        functools.partial(body, axes),
        mesh=mesh,
        in_specs=(P(*axes), P(*axes), P(), P(*axes), P(*axes)),
        out_specs=(P(*axes), P(*axes)),
        check_vma=False,
    )
```

```python
import functools
import math

import jax
import jax.numpy as jnp
import numpy as np
from jax import lax
from jax.experimental import pallas as pl
from jax.experimental.pallas import tpu as pltpu
from jax.sharding import PartitionSpec as P

HALO = 64
FREQS = 64
ITERS = 2
STEP_SIZE = 0.05
STEEPNESS = 4.0
THRESHOLD = 1.0
YBLOCK = 64
FLAG_LANE = FREQS + FREQS // 2

DIRS = [(1, 1), (-1, -1), (1, -1), (-1, 1), (1, 0), (-1, 0), (0, 1), (0, -1)]


def slot(di, dj):
    return 3 * (di % 3) + dj % 3


def make_tables(core, tile):
    bf16 = jnp.bfloat16
    place = (np.arange(tile) + HALO) % tile
    frequency = np.arange(FREQS) - FREQS // 2

    def waves(position):
        angle = (frequency[None, :] * position[:, None] % tile) * (2.0 * math.pi / tile)
        return np.concatenate([np.cos(angle), np.sin(angle)], 1)

    whole = waves(place).astype(np.float32)

    def split(table):
        table = table.astype(np.float32)
        high = table.astype(bf16)
        return high, (table - high.astype(np.float32)).astype(bf16)

    below = waves(place - core) * (place >= core)[:, None]
    above = waves(place + core) * (place < 2 * HALO)[:, None]
    spread = np.concatenate([whole, below, above], 1).astype(np.float32)
    samples = np.arange(2 * FREQS) * (tile // (2 * FREQS))
    wave_high, wave_low = split(waves(samples))
    apart = place[:core, None] - samples[None, :]
    difference = np.arange(1, FREQS)
    turns = difference[:, None, None] * apart[None] % tile * (2.0 * math.pi / tile)
    interpolate = (1.0 + 2.0 * np.cos(turns).sum(0)) / (2 * FREQS)
    fine_high, fine_low = split(interpolate)
    return dict(
        forward=np.ascontiguousarray((whole / tile).T).astype(bf16),
        whole=np.concatenate(split(whole)[:1] * 2 + split(whole)[1:], 0),
        half=np.concatenate([wave_high, wave_low], 1),
        inverse_t=np.concatenate([wave_high.T, wave_low.T], 0),
        inverse=wave_high,
        half_t=np.concatenate([wave_high.T, wave_low.T], 1),
        fine=np.concatenate([fine_high, fine_low, fine_high], 1),
        fine_t=np.concatenate([fine_high.T, fine_high.T, fine_low.T], 0),
        rows=spread.astype(bf16),
        cols=np.ascontiguousarray((spread / tile).T).astype(bf16),
    )


def halves(value):
    high = value.astype(jnp.bfloat16)
    return high, (value - high.astype(jnp.float32)).astype(jnp.bfloat16)


def whole_of(high, low):
    return high.astype(jnp.float32) + low.astype(jnp.float32)


def pack_side(block, right):
    half = block.shape[0] // 2
    upper, lower = block[:half], block[half:]
    if right:
        return jnp.where(left_lanes(), pltpu.roll(upper, FREQS, 1), lower)
    return jnp.where(left_lanes(), upper, pltpu.roll(lower, FREQS, 1))


def join_sides(from_right, from_left):
    upper = jnp.where(left_lanes(), from_right, pltpu.roll(from_left, FREQS, 1))
    lower = jnp.where(left_lanes(), pltpu.roll(from_right, FREQS, 1), from_left)
    return jnp.concatenate([upper, lower], 0)


def side_parts(core):
    whole, corner = core // 2, HALO // 2
    return {0: (0, whole), -1: (whole, corner), 1: (whole + corner, corner)}


def bands(core):
    return ((0, core), (core, HALO), (core + HALO, HALO))


def left_lanes():
    return lax.broadcasted_iota(jnp.int32, (1, 128), 1) < FREQS


def band_gradient(slots, blocks, rows_ref, cols_ref, loads=()):
    f32, bf16 = jnp.float32, jnp.bfloat16
    for gi in range(3):
        for gj in range(3):
            top = slots[3 * gi + gj].astype(f32)
            turned = pltpu.roll(top, FREQS, 1)
            low = jnp.where(left_lanes(), turned, -turned)
            blocks[gj * 128 : gj * 128 + 128, gi * 128 : gi * 128 + 128] = jnp.concatenate(
                [top, low], 0
            ).astype(bf16)
    for load in loads:
        load.wait()
    spread = lax.dot_general(
        rows_ref[...], blocks[...], (((1,), (1,)), ((), ())), preferred_element_type=f32
    ).astype(bf16)
    return jnp.dot(spread, cols_ref[...], preferred_element_type=f32)


def flag_row(slots, gi, core):
    at = FREQS // 2
    here = lax.broadcasted_iota(jnp.int32, (1, 128), 1) == FLAG_LANE
    flags = [slots[3 * gi + gj, at : at + 16, :].astype(jnp.float32)[:1] for gj in range(3)]
    flags = [jnp.sum(jnp.where(here, flag, 0.0), axis=1, keepdims=True) for flag in flags]
    flags = [jnp.broadcast_to(flag, (1, 128)) for flag in flags]
    sides = jnp.where(left_lanes(), flags[1], flags[2])
    return jnp.concatenate([flags[0]] * (core // 128) + [sides], 1)


def finish(
    last_ref, rows_src, cols_src, window_ref, final_ref, next_ref,
    last, rows, cols, window, blocks, final, following, load_sems, store_sems,
):
    loads = [
        pltpu.make_async_copy(source, target, load_sems.at[at])
        for at, (source, target) in enumerate(
            ((last_ref, last), (rows_src, rows), (cols_src, cols), (window_ref, window))
        )
    ]
    for load in loads:
        load.start()
    core, tile = final.shape[0], following.shape[0]
    loads[0].wait()
    total = band_gradient(last, blocks, rows, cols, loads[1:3])
    loads[3].wait()
    stores = []
    for gi, (start, size) in enumerate(bands(core)):
        at = slice(start, start + size)
        scale = flag_row(last, gi, core)
        fresh = jnp.clip(window[at, :] - STEP_SIZE * scale * total[at], -1.0, 1.0)
        out = pl.ds((start + HALO) % tile, size)
        following[out, :] = pltpu.roll(fresh, HALO, 1)
        stores.append(
            pltpu.make_async_copy(following.at[out, :], next_ref.at[out, :], store_sems.at[gi])
        )
        stores[-1].start()
        if gi == 0:
            final[...] = fresh[:, :core]
            stores.append(pltpu.make_async_copy(final, final_ref, store_sems.at[3]))
            stores[-1].start()
    for store in stores:
        store.wait()


def kernel(axes, count, colour_ref, active_ref, *refs):
    sources, (window_ref, last_ref) = refs[:count], refs[count : count + 2]
    held = refs[count + 2 : 2 * count + 2]
    run(axes, colour_ref, active_ref, sources, held, window_ref, last_ref, *refs[2 * count + 2 :])


def run(
    axes,
    colour_ref,
    active_ref,
    sources,
    held,
    window_ref,
    last_ref,
    mask16,
    rest16,
    pack16,
    pack_rest,
    vert16,
    side16,
    vert_rest,
    side_rest,
    window,
    image,
    grads,
    blocks,
    ka,
    kc,
    goal_t,
    weights,
    d_half,
    intensity,
    d_intensity,
    send_sems,
    recv_sems,
    load_sems,
    keep_sems,
):
    loads = [
        pltpu.make_async_copy(source, target, load_sems.at[at])
        for at, (source, target) in enumerate(zip(sources, held))
    ]
    loads[0].start()
    mask_ref, goal_ref, kern_ref, forward_ref, whole_ref, half_ref = held[:6]
    inverse_t_ref, inverse_ref, half_t_ref, fine_ref, fine_t_ref, rows_ref, cols_ref = held[6:]
    core = mask_ref.shape[0]
    tile = core + 2 * HALO
    kerns = ka.shape[0]
    f32, bf16 = jnp.float32, jnp.bfloat16
    n_row, n_col = lax.axis_size(axes[0]), lax.axis_size(axes[1])
    row, col = lax.axis_index(axes[0]), lax.axis_index(axes[1])

    def exists(di, dj):
        there = (row + di >= 0) & (row + di < n_row)
        return there & (col + dj >= 0) & (col + dj < n_col)

    barrier = pltpu.get_barrier_semaphore()
    for di, dj in DIRS:

        @pl.when(exists(di, dj))
        def _(di=di, dj=dj):
            pl.semaphore_signal(
                barrier, inc=1, device_id=(row + di, col + dj), device_id_type=pl.DeviceIdType.MESH
            )

    first = (mask16, pack16, vert16, side16)
    second = (rest16, pack_rest, vert_rest, side_rest)

    def halo_refs(di, dj, source, packed, vert, side):
        if dj == 0:
            rows = pl.ds(core - HALO, HALO) if di == 1 else pl.ds(0, HALO)
            return source.at[rows, :], vert.at[1 if di == 1 else 0]
        at = pl.ds(*side_parts(core)[di])
        return packed.at[1 if dj == 1 else 0, at, :], side.at[1 if dj == 1 else 0, at, :]

    def slots_of(step):
        return last_ref if step == ITERS - 1 else grads.at[step]

    def blank(di, dj):
        at = slot(di, dj)
        return pltpu.make_async_copy(grads.at[ITERS - 1, at], last_ref.at[at], keep_sems.at[at])

    keep_own = pltpu.make_async_copy(grads.at[ITERS - 1, 0], last_ref.at[0], keep_sems.at[0])
    keep_window = pltpu.make_async_copy(window, window_ref, keep_sems.at[9])

    def message(phase, di, dj, target):
        if phase < 2:
            pair = first if phase == 0 else second
            source, land = halo_refs(di, dj, *pair)
        else:
            source, land = grads.at[phase - 2, 0], slots_of(phase - 2).at[slot(-di, -dj)]
        return pltpu.make_async_remote_copy(
            src_ref=source,
            dst_ref=land,
            send_sem=send_sems.at[phase, slot(di, dj)],
            recv_sem=recv_sems.at[phase, slot(di, dj)],
            device_id=target,
            device_id_type=pl.DeviceIdType.MESH,
        )

    def send(phase):
        for di, dj in DIRS:

            @pl.when(exists(di, dj))
            def _(di=di, dj=dj):
                message(phase, di, dj, (row + di, col + dj)).start()

    def wait_arrivals(phase):
        for di, dj in DIRS:

            @pl.when(exists(-di, -dj))
            def _(di=di, dj=dj):
                message(phase, di, dj, (row - di, col - dj)).wait_recv()

    def wait_sent(phase):
        for di, dj in DIRS:

            @pl.when(exists(di, dj))
            def _(di=di, dj=dj):
                message(phase, di, dj, (row + di, col + dj)).wait_send()

    loads[0].wait()
    for load in loads[1:]:
        load.start()
    def pack(source, packed):
        for right in (0, 1):
            lanes = slice(core - 128, core) if right else slice(0, 128)
            for di, rows in ((0, slice(0, core)), (-1, slice(0, HALO)), (1, slice(core - HALO, core))):
                start, size = side_parts(core)[di]
                part = pack_side(source[rows, lanes].astype(f32), right)
                packed[right, start : start + size, :] = part.astype(bf16)

    def unpack(side):
        parts = [side_parts(core)[di] for di in (0, -1, 1)]
        return jnp.concatenate(
            [join_sides(*[side[at, p : p + n, :].astype(f32) for at in (0, 1)]) for p, n in parts], 0
        )

    mask16[...] = mask_ref[...].astype(bf16)
    pack(mask16, pack16)
    for di, dj in DIRS:

        @pl.when(jnp.logical_not(exists(di, dj)))
        def _(di=di, dj=dj):
            for pair in (first, second):
                _, land = halo_refs(-di, -dj, *pair)
                land[...] = jnp.zeros(land.shape, land.dtype)
            for step in range(ITERS):
                spot = grads.at[step, slot(di, dj)]
                spot[...] = jnp.zeros(spot.shape, spot.dtype)
            blank(di, dj).start()

    peers = sum(exists(di, dj).astype(jnp.int32) for di, dj in DIRS)
    pl.semaphore_wait(barrier, peers)

    send(0)
    rest16[...] = (mask_ref[...] - mask16[...].astype(f32)).astype(bf16)
    pack(rest16, pack_rest)

    for load in loads[1:]:
        load.wait()
    goal_t[...] = goal_ref[...].T
    for k in range(kerns):
        real, imag = kern_ref[k, :FREQS, :], kern_ref[k, FREQS:, :]
        ka[k] = jnp.concatenate([real, -imag], 0).T
        kc[k] = jnp.concatenate([imag, real], 0).T
    update = jnp.where(colour_ref[0, 0] == 0, 1.0, 0.0).astype(f32)
    active = active_ref[0, 0].astype(f32)
    left_half = lax.broadcasted_iota(jnp.int32, (1, 128), 1) < FREQS
    flag_spot = lax.broadcasted_iota(jnp.int32, (FREQS, 128), 0) == FREQS // 2
    flag_spot &= lax.broadcasted_iota(jnp.int32, (FREQS, 128), 1) == FLAG_LANE

    image[:core, :core] = mask16[...]
    window[:core, :core] = mask_ref[...]

    for step in range(ITERS):
        if step == 0:
            wait_arrivals(0)
            send(1)
            image[core : core + HALO, :core] = vert16[0]
            image[core + HALO :, :core] = vert16[1]
            image[:, core:] = unpack(side16).astype(bf16)
        else:
            image[...] = window[...].astype(bf16)

        partial = lax.dot_general(
            forward_ref[...], image[...], (((1,), (1,)), ((), ())), preferred_element_type=f32
        )
        high, low = halves(partial)
        quads = jnp.dot(
            jnp.concatenate([high, low, high], 1), whole_ref[...], preferred_element_type=f32
        ) * (1.0 / tile)
        upper, lower = quads[:FREQS], quads[FREQS:]
        real = upper - pltpu.roll(lower, FREQS, 1)
        imag = -(lower + pltpu.roll(upper, FREQS, 1))
        real = jnp.where(left_half, real, pltpu.roll(real, FREQS, 1))
        imag = jnp.where(left_half, imag, pltpu.roll(imag, FREQS, 1))

        for k in range(kerns):
            x = ka[k] * real - kc[k] * imag
            y = kc[k] * real + ka[k] * imag
            both = jnp.concatenate([jnp.concatenate([x, -y], 0), jnp.concatenate([y, x], 0)], 1)
            high = both.astype(bf16)
            at = pl.ds(k * 256, 256)
            weights[:128, at] = high
            weights[128:, at] = high
        halfway = jnp.dot(half_ref[...], weights[...], preferred_element_type=f32).astype(bf16)
        pieces = [slice(kp * 128, (kp + 1) * 128) for kp in range(2 * kerns)]
        stacked = jnp.concatenate([halfway[:, at] for at in pieces], 0)
        fields = jnp.dot(
            jnp.concatenate([stacked, stacked], 1), inverse_t_ref[...], preferred_element_type=f32
        ).reshape(2 * kerns, 2 * FREQS, 2 * FREQS)
        high, low = halves(jnp.sum(fields * fields, axis=0))
        across = jnp.dot(
            jnp.concatenate([high, low, high], 1), fine_t_ref[...], preferred_element_type=f32
        )
        high, low = halves(across)
        intensity[...] = jnp.dot(
            fine_ref[...], jnp.concatenate([high, high, low], 0), preferred_element_type=f32
        )
        for start in range(0, core, YBLOCK):
            at = slice(start, start + YBLOCK)
            resist = 1.0 / (1.0 + jnp.exp(-STEEPNESS * (intensity[at, :] - THRESHOLD)))
            slope = (4.0 * STEEPNESS) * (resist - goal_t[at, :]) * (resist * (1.0 - resist))
            d_intensity[at, :] = slope.astype(bf16)
        d_across = jnp.dot(
            fine_t_ref[: 2 * FREQS, :], d_intensity[...], preferred_element_type=f32
        ).astype(bf16)
        d_samples = jnp.dot(d_across, fine_ref[:, : 2 * FREQS], preferred_element_type=f32)
        d_fields = (fields * d_samples[None]).astype(bf16).reshape(-1, 2 * FREQS)
        back = jnp.dot(d_fields, inverse_ref[...], preferred_element_type=f32).astype(bf16)
        for kp, at in enumerate(pieces):
            piece = back[kp * 128 : (kp + 1) * 128]
            d_half[:128, at] = piece
            d_half[128:, at] = piece

        d_weights = jnp.dot(half_t_ref[...], d_half[...], preferred_element_type=f32)
        d_real = jnp.zeros((FREQS, 128), f32)
        d_imag = jnp.zeros((FREQS, 128), f32)
        for k in range(kerns):
            at = k * 256
            dx = d_weights[:FREQS, at : at + 128] + d_weights[FREQS:, at + 128 : at + 256]
            dy = d_weights[:FREQS, at + 128 : at + 256] - d_weights[FREQS:, at : at + 128]
            d_real += ka[k] * dx + kc[k] * dy
            d_imag += ka[k] * dy - kc[k] * dx
        d_real = d_real + pltpu.roll(d_real, FREQS, 1)
        d_imag = d_imag + pltpu.roll(d_imag, FREQS, 1)
        own = jnp.where(left_half, d_real, -d_imag) * (active * (1.0 / tile))
        grads[step, 0] = jnp.where(flag_spot, update, own).astype(bf16)
        send(2 + step)
        if step == ITERS - 1:
            keep_own.start()
            keep_window.start()
        if step == 0:
            wait_arrivals(1)
            for at in (0, 1):
                start = core + at * HALO
                window[start : start + HALO, :core] = whole_of(vert16[at], vert_rest[at])
            window[:, core:] = unpack(side16) + unpack(side_rest)
        wait_arrivals(2 + step)

        if step < ITERS - 1:
            total = band_gradient(grads.at[step], blocks, rows_ref, cols_ref)
            for gi, (start, size) in enumerate(bands(core)):
                at = slice(start, start + size)
                scale = flag_row(grads.at[step], gi, core)
                window[at, :] = jnp.clip(window[at, :] - STEP_SIZE * scale * total[at], -1.0, 1.0)
    keep_window.wait()
    keep_own.wait()
    for di, dj in DIRS:

        @pl.when(jnp.logical_not(exists(di, dj)))
        def _(di=di, dj=dj):
            blank(di, dj).wait()

    for phase in range(2 + ITERS):
        wait_sent(phase)


def body(axes, mask_field, resist_goal, kernels, colour, active):
    core = mask_field.shape[0]
    tile = core + 2 * HALO
    kerns = kernels.shape[0]
    tables = make_tables(core, tile)
    f32, bf16 = jnp.float32, jnp.bfloat16
    sources = [mask_field, resist_goal, kernels.reshape(kerns, 2 * FREQS, FREQS)]
    sources += [jnp.asarray(table) for table in tables.values()]
    hbm = pl.BlockSpec(memory_space=pltpu.HBM)
    smem = pl.BlockSpec(memory_space=pltpu.SMEM)
    window, last = pl.pallas_call(
        functools.partial(kernel, axes, len(sources)),
        out_shape=(
            jax.ShapeDtypeStruct((tile, tile), f32),
            jax.ShapeDtypeStruct((9, FREQS, 128), bf16),
        ),
        in_specs=[smem, smem] + [hbm] * len(sources),
        out_specs=(hbm, hbm),
        scratch_shapes=[pltpu.VMEM(source.shape, source.dtype) for source in sources]
        + [
            pltpu.VMEM((core, core), bf16),
            pltpu.VMEM((core, core), bf16),
            pltpu.VMEM((2, tile // 2, 128), bf16),
            pltpu.VMEM((2, tile // 2, 128), bf16),
            pltpu.VMEM((2, HALO, core), bf16),
            pltpu.VMEM((2, tile // 2, 128), bf16),
            pltpu.VMEM((2, HALO, core), bf16),
            pltpu.VMEM((2, tile // 2, 128), bf16),
            pltpu.VMEM((tile, tile), f32),
            pltpu.VMEM((tile, tile), bf16),
            pltpu.VMEM((ITERS, 9, FREQS, 128), bf16),
            pltpu.VMEM((384, 384), bf16),
            pltpu.VMEM((kerns, FREQS, 128), f32),
            pltpu.VMEM((kerns, FREQS, 128), f32),
            pltpu.VMEM((core, core), f32),
            pltpu.VMEM((256, kerns * 256), bf16),
            pltpu.VMEM((256, kerns * 256), bf16),
            pltpu.VMEM((core, core), f32),
            pltpu.VMEM((core, core), bf16),
            pltpu.SemaphoreType.DMA((2 + ITERS, 9)),
            pltpu.SemaphoreType.DMA((2 + ITERS, 9)),
            pltpu.SemaphoreType.DMA((len(sources),)),
            pltpu.SemaphoreType.DMA((10,)),
        ],
        compiler_params=pltpu.CompilerParams(
            collective_id=0, has_side_effects=True, vmem_limit_bytes=56 * 1024 * 1024
        ),
    )(
        colour,
        active,
        *sources,
    )
    finals = [last, sources[-2], sources[-1], window]
    return pl.pallas_call(
        finish,
        out_shape=(
            jax.ShapeDtypeStruct((core, core), f32),
            jax.ShapeDtypeStruct((tile, tile), f32),
        ),
        in_specs=[hbm] * len(finals),
        out_specs=(hbm, hbm),
        scratch_shapes=[pltpu.VMEM(source.shape, source.dtype) for source in finals]
        + [
            pltpu.VMEM((384, 384), bf16),
            pltpu.VMEM((core, core), f32),
            pltpu.VMEM((tile, tile), f32),
            pltpu.SemaphoreType.DMA((4,)),
            pltpu.SemaphoreType.DMA((4,)),
        ],
        compiler_params=pltpu.CompilerParams(vmem_limit_bytes=56 * 1024 * 1024),
    )(*finals)


def solution(mesh):
    axes = mesh.axis_names
    return jax.shard_map(
        functools.partial(body, axes),
        mesh=mesh,
        in_specs=(P(*axes), P(*axes), P(), P(*axes), P(*axes)),
        out_specs=(P(*axes), P(*axes)),
        check_vma=False,
    )
```

```python
import functools
import math

import jax
import jax.numpy as jnp
import numpy as np
from jax import lax
from jax.experimental import pallas as pl
from jax.experimental.pallas import tpu as pltpu
from jax.sharding import PartitionSpec as P

HALO = 64
FREQS = 64
ITERS = 2
STEP_SIZE = 0.05
STEEPNESS = 4.0
THRESHOLD = 1.0
YBLOCK = 64
FLAG_LANE = FREQS + FREQS // 2

DIRS = [(1, 1), (-1, -1), (1, -1), (-1, 1), (1, 0), (-1, 0), (0, 1), (0, -1)]


def slot(di, dj):
    return 3 * (di % 3) + dj % 3


def make_tables(core, tile):
    bf16 = jnp.bfloat16
    place = (np.arange(tile) + HALO) % tile
    frequency = np.arange(FREQS) - FREQS // 2

    def waves(position):
        angle = (frequency[None, :] * position[:, None] % tile) * (2.0 * math.pi / tile)
        return np.concatenate([np.cos(angle), np.sin(angle)], 1)

    whole = waves(place).astype(np.float32)

    def split(table):
        table = table.astype(np.float32)
        high = table.astype(bf16)
        return high, (table - high.astype(np.float32)).astype(bf16)

    below = waves(place - core) * (place >= core)[:, None]
    above = waves(place + core) * (place < 2 * HALO)[:, None]
    spread = np.concatenate([whole, below, above], 1).astype(np.float32)
    samples = np.arange(2 * FREQS) * (tile // (2 * FREQS))
    wave_high, wave_low = split(waves(samples))
    apart = place[:core, None] - samples[None, :]
    difference = np.arange(1, FREQS)
    turns = difference[:, None, None] * apart[None] % tile * (2.0 * math.pi / tile)
    interpolate = (1.0 + 2.0 * np.cos(turns).sum(0)) / (2 * FREQS)
    fine_high, fine_low = split(interpolate)
    return dict(
        forward=np.ascontiguousarray((whole / tile).T).astype(bf16),
        whole=np.concatenate(split(whole)[:1] * 2 + split(whole)[1:], 0),
        half=np.concatenate([wave_high, wave_low], 1),
        inverse_t=np.concatenate([wave_high.T, wave_low.T], 0),
        inverse=wave_high,
        half_t=np.concatenate([wave_high.T, wave_low.T], 1),
        fine=np.concatenate([fine_high, fine_low, fine_high], 1),
        fine_t=np.concatenate([fine_high.T, fine_high.T, fine_low.T], 0),
        rows=spread.astype(bf16),
        cols=np.ascontiguousarray((spread / tile).T).astype(bf16),
    )


def halves(value):
    high = value.astype(jnp.bfloat16)
    return high, (value - high.astype(jnp.float32)).astype(jnp.bfloat16)


def whole_of(high, low):
    return high.astype(jnp.float32) + low.astype(jnp.float32)


def pack_side(block, right):
    half = block.shape[0] // 2
    upper, lower = block[:half], block[half:]
    if right:
        return jnp.where(left_lanes(), pltpu.roll(upper, FREQS, 1), lower)
    return jnp.where(left_lanes(), upper, pltpu.roll(lower, FREQS, 1))


def join_sides(from_right, from_left):
    upper = jnp.where(left_lanes(), from_right, pltpu.roll(from_left, FREQS, 1))
    lower = jnp.where(left_lanes(), pltpu.roll(from_right, FREQS, 1), from_left)
    return jnp.concatenate([upper, lower], 0)


def side_parts(core):
    whole, corner = core // 2, HALO // 2
    return {0: (0, whole), -1: (whole, corner), 1: (whole + corner, corner)}


def bands(core):
    return ((0, core), (core, HALO), (core + HALO, HALO))


def left_lanes():
    return lax.broadcasted_iota(jnp.int32, (1, 128), 1) < FREQS


def band_gradient(slots, blocks, rows_ref, loads=()):
    f32, bf16 = jnp.float32, jnp.bfloat16
    for gi in range(3):
        for gj in range(3):
            top = slots[3 * gi + gj].astype(f32)
            turned = pltpu.roll(top, FREQS, 1)
            low = jnp.where(left_lanes(), turned, -turned)
            blocks[gj * 128 : gj * 128 + 128, gi * 128 : gi * 128 + 128] = jnp.concatenate(
                [top, low], 0
            ).astype(bf16)
    for load in loads:
        load.wait()
    spread = lax.dot_general(
        rows_ref[...], blocks[...], (((1,), (1,)), ((), ())), preferred_element_type=f32
    ).astype(bf16)
    return spread


def flag_row(slots, gi, core):
    at = FREQS // 2
    here = lax.broadcasted_iota(jnp.int32, (1, 128), 1) == FLAG_LANE
    flags = [slots[3 * gi + gj, at : at + 16, :].astype(jnp.float32)[:1] for gj in range(3)]
    flags = [jnp.sum(jnp.where(here, flag, 0.0), axis=1, keepdims=True) for flag in flags]
    flags = [jnp.broadcast_to(flag, (1, 128)) for flag in flags]
    sides = jnp.where(left_lanes(), flags[1], flags[2])
    return jnp.concatenate([flags[0]] * (core // 128) + [sides], 1)


def finish(
    last_ref, rows_src, cols_src, window_ref, final_ref, next_ref,
    last, rows, cols, window, blocks, final, following, load_sems, store_sems,
):
    loads = [
        pltpu.make_async_copy(source, target, load_sems.at[at])
        for at, (source, target) in enumerate(
            ((last_ref, last), (rows_src, rows), (cols_src, cols), (window_ref, window))
        )
    ]
    for load in loads:
        load.start()
    core, tile = final.shape[0], following.shape[0]
    loads[0].wait()
    spread = band_gradient(last, blocks, rows, loads[1:2])
    loads[2].wait()
    loads[3].wait()
    stores = []
    for gi, (start, size) in enumerate(bands(core)):
        at = slice(start, start + size)
        scale = flag_row(last, gi, core)
        if gi < 2:
            below = slice(0, core) if gi == 0 else slice(core, tile)
            part = jnp.dot(spread[below], cols[...], preferred_element_type=jnp.float32)
        total = part if gi == 0 else part[start - core : start - core + size]
        fresh = jnp.clip(window[at, :] - STEP_SIZE * scale * total, -1.0, 1.0)
        out = pl.ds((start + HALO) % tile, size)
        following[out, :] = pltpu.roll(fresh, HALO, 1)
        stores.append(
            pltpu.make_async_copy(following.at[out, :], next_ref.at[out, :], store_sems.at[gi])
        )
        stores[-1].start()
        if gi == 0:
            final[...] = fresh[:, :core]
            stores.append(pltpu.make_async_copy(final, final_ref, store_sems.at[3]))
            stores[-1].start()
    for store in stores:
        store.wait()


def kernel(axes, count, colour_ref, active_ref, *refs):
    sources, (window_ref, last_ref) = refs[:count], refs[count : count + 2]
    held = refs[count + 2 : 2 * count + 2]
    run(axes, colour_ref, active_ref, sources, held, window_ref, last_ref, *refs[2 * count + 2 :])


def run(
    axes,
    colour_ref,
    active_ref,
    sources,
    held,
    window_ref,
    last_ref,
    mask16,
    rest16,
    pack16,
    pack_rest,
    vert16,
    side16,
    vert_rest,
    side_rest,
    window,
    image,
    grads,
    blocks,
    ka,
    kc,
    goal_t,
    weights,
    d_half,
    intensity,
    d_intensity,
    send_sems,
    recv_sems,
    load_sems,
    keep_sems,
):
    loads = [
        pltpu.make_async_copy(source, target, load_sems.at[at])
        for at, (source, target) in enumerate(zip(sources, held))
    ]
    loads[0].start()
    mask_ref, goal_ref, kern_ref, forward_ref, whole_ref, half_ref = held[:6]
    inverse_t_ref, inverse_ref, half_t_ref, fine_ref, fine_t_ref, rows_ref, cols_ref = held[6:]
    core = mask_ref.shape[0]
    tile = core + 2 * HALO
    kerns = ka.shape[0]
    f32, bf16 = jnp.float32, jnp.bfloat16
    n_row, n_col = lax.axis_size(axes[0]), lax.axis_size(axes[1])
    row, col = lax.axis_index(axes[0]), lax.axis_index(axes[1])

    def exists(di, dj):
        there = (row + di >= 0) & (row + di < n_row)
        return there & (col + dj >= 0) & (col + dj < n_col)

    barrier = pltpu.get_barrier_semaphore()
    for di, dj in DIRS:

        @pl.when(exists(di, dj))
        def _(di=di, dj=dj):
            pl.semaphore_signal(
                barrier, inc=1, device_id=(row + di, col + dj), device_id_type=pl.DeviceIdType.MESH
            )

    first = (mask16, pack16, vert16, side16)
    second = (rest16, pack_rest, vert_rest, side_rest)

    def halo_refs(di, dj, source, packed, vert, side):
        if dj == 0:
            rows = pl.ds(core - HALO, HALO) if di == 1 else pl.ds(0, HALO)
            return source.at[rows, :], vert.at[1 if di == 1 else 0]
        at = pl.ds(*side_parts(core)[di])
        return packed.at[1 if dj == 1 else 0, at, :], side.at[1 if dj == 1 else 0, at, :]

    def slots_of(step):
        return last_ref if step == ITERS - 1 else grads.at[step]

    def blank(di, dj):
        at = slot(di, dj)
        return pltpu.make_async_copy(grads.at[ITERS - 1, at], last_ref.at[at], keep_sems.at[at])

    keep_own = pltpu.make_async_copy(grads.at[ITERS - 1, 0], last_ref.at[0], keep_sems.at[0])
    keep_window = pltpu.make_async_copy(window, window_ref, keep_sems.at[9])

    def message(phase, di, dj, target):
        if phase < 2:
            pair = first if phase == 0 else second
            source, land = halo_refs(di, dj, *pair)
        else:
            source, land = grads.at[phase - 2, 0], slots_of(phase - 2).at[slot(-di, -dj)]
        return pltpu.make_async_remote_copy(
            src_ref=source,
            dst_ref=land,
            send_sem=send_sems.at[phase, slot(di, dj)],
            recv_sem=recv_sems.at[phase, slot(di, dj)],
            device_id=target,
            device_id_type=pl.DeviceIdType.MESH,
        )

    def send(phase):
        for di, dj in DIRS:

            @pl.when(exists(di, dj))
            def _(di=di, dj=dj):
                message(phase, di, dj, (row + di, col + dj)).start()

    def wait_arrivals(phase):
        for di, dj in DIRS:

            @pl.when(exists(-di, -dj))
            def _(di=di, dj=dj):
                message(phase, di, dj, (row - di, col - dj)).wait_recv()

    def wait_sent(phase):
        for di, dj in DIRS:

            @pl.when(exists(di, dj))
            def _(di=di, dj=dj):
                message(phase, di, dj, (row + di, col + dj)).wait_send()

    loads[0].wait()
    for load in loads[1:]:
        load.start()
    def pack(source, packed):
        for right in (0, 1):
            lanes = slice(core - 128, core) if right else slice(0, 128)
            for di, rows in ((0, slice(0, core)), (-1, slice(0, HALO)), (1, slice(core - HALO, core))):
                start, size = side_parts(core)[di]
                part = pack_side(source[rows, lanes].astype(f32), right)
                packed[right, start : start + size, :] = part.astype(bf16)

    def unpack(side):
        parts = [side_parts(core)[di] for di in (0, -1, 1)]
        return jnp.concatenate(
            [join_sides(*[side[at, p : p + n, :].astype(f32) for at in (0, 1)]) for p, n in parts], 0
        )

    mask16[...] = mask_ref[...].astype(bf16)
    pack(mask16, pack16)
    for di, dj in DIRS:

        @pl.when(jnp.logical_not(exists(di, dj)))
        def _(di=di, dj=dj):
            for pair in (first, second):
                _, land = halo_refs(-di, -dj, *pair)
                land[...] = jnp.zeros(land.shape, land.dtype)
            for step in range(ITERS):
                spot = grads.at[step, slot(di, dj)]
                spot[...] = jnp.zeros(spot.shape, spot.dtype)
            blank(di, dj).start()

    peers = sum(exists(di, dj).astype(jnp.int32) for di, dj in DIRS)
    pl.semaphore_wait(barrier, peers)

    send(0)
    rest16[...] = (mask_ref[...] - mask16[...].astype(f32)).astype(bf16)
    pack(rest16, pack_rest)

    for load in loads[1:]:
        load.wait()
    goal_t[...] = goal_ref[...].T
    for k in range(kerns):
        real, imag = kern_ref[k, :FREQS, :], kern_ref[k, FREQS:, :]
        ka[k] = jnp.concatenate([real, -imag], 0).T
        kc[k] = jnp.concatenate([imag, real], 0).T
    update = jnp.where(colour_ref[0, 0] == 0, 1.0, 0.0).astype(f32)
    active = active_ref[0, 0].astype(f32)
    left_half = lax.broadcasted_iota(jnp.int32, (1, 128), 1) < FREQS
    flag_spot = lax.broadcasted_iota(jnp.int32, (FREQS, 128), 0) == FREQS // 2
    flag_spot &= lax.broadcasted_iota(jnp.int32, (FREQS, 128), 1) == FLAG_LANE

    image[:core, :core] = mask16[...]
    window[:core, :core] = mask_ref[...]

    for step in range(ITERS):
        if step == 0:
            wait_arrivals(0)
            send(1)
            image[core : core + HALO, :core] = vert16[0]
            image[core + HALO :, :core] = vert16[1]
            image[:, core:] = unpack(side16).astype(bf16)
        else:
            image[...] = window[...].astype(bf16)

        partial = lax.dot_general(
            forward_ref[...], image[...], (((1,), (1,)), ((), ())), preferred_element_type=f32
        )
        high, low = halves(partial)
        quads = jnp.dot(
            jnp.concatenate([high, low, high], 1), whole_ref[...], preferred_element_type=f32
        ) * (1.0 / tile)
        upper, lower = quads[:FREQS], quads[FREQS:]
        real = upper - pltpu.roll(lower, FREQS, 1)
        imag = -(lower + pltpu.roll(upper, FREQS, 1))
        real = jnp.where(left_half, real, pltpu.roll(real, FREQS, 1))
        imag = jnp.where(left_half, imag, pltpu.roll(imag, FREQS, 1))

        for k in range(kerns):
            x = ka[k] * real - kc[k] * imag
            y = kc[k] * real + ka[k] * imag
            both = jnp.concatenate([jnp.concatenate([x, -y], 0), jnp.concatenate([y, x], 0)], 1)
            high = both.astype(bf16)
            at = pl.ds(k * 256, 256)
            weights[:128, at] = high
            weights[128:, at] = high
        halfway = jnp.dot(half_ref[...], weights[...], preferred_element_type=f32).astype(bf16)
        pieces = [slice(kp * 128, (kp + 1) * 128) for kp in range(2 * kerns)]
        stacked = jnp.concatenate([halfway[:, at] for at in pieces], 0)
        fields = jnp.dot(
            jnp.concatenate([stacked, stacked], 1), inverse_t_ref[...], preferred_element_type=f32
        ).reshape(2 * kerns, 2 * FREQS, 2 * FREQS)
        high, low = halves(jnp.sum(fields * fields, axis=0))
        across = jnp.dot(
            jnp.concatenate([high, low, high], 1), fine_t_ref[...], preferred_element_type=f32
        )
        high, low = halves(across)
        intensity[...] = jnp.dot(
            fine_ref[...], jnp.concatenate([high, high, low], 0), preferred_element_type=f32
        )
        for start in range(0, core, YBLOCK):
            at = slice(start, start + YBLOCK)
            resist = 1.0 / (1.0 + jnp.exp(-STEEPNESS * (intensity[at, :] - THRESHOLD)))
            slope = (4.0 * STEEPNESS) * (resist - goal_t[at, :]) * (resist * (1.0 - resist))
            d_intensity[at, :] = slope.astype(bf16)
        d_across = jnp.dot(
            fine_t_ref[: 2 * FREQS, :], d_intensity[...], preferred_element_type=f32
        ).astype(bf16)
        d_samples = jnp.dot(d_across, fine_ref[:, : 2 * FREQS], preferred_element_type=f32)
        d_fields = (fields * d_samples[None]).astype(bf16).reshape(-1, 2 * FREQS)
        back = jnp.dot(d_fields, inverse_ref[...], preferred_element_type=f32).astype(bf16)
        for kp, at in enumerate(pieces):
            piece = back[kp * 128 : (kp + 1) * 128]
            d_half[:128, at] = piece
            d_half[128:, at] = piece

        d_weights = jnp.dot(half_t_ref[...], d_half[...], preferred_element_type=f32)
        d_real = jnp.zeros((FREQS, 128), f32)
        d_imag = jnp.zeros((FREQS, 128), f32)
        for k in range(kerns):
            at = k * 256
            dx = d_weights[:FREQS, at : at + 128] + d_weights[FREQS:, at + 128 : at + 256]
            dy = d_weights[:FREQS, at + 128 : at + 256] - d_weights[FREQS:, at : at + 128]
            d_real += ka[k] * dx + kc[k] * dy
            d_imag += ka[k] * dy - kc[k] * dx
        d_real = d_real + pltpu.roll(d_real, FREQS, 1)
        d_imag = d_imag + pltpu.roll(d_imag, FREQS, 1)
        own = jnp.where(left_half, d_real, -d_imag) * (active * (1.0 / tile))
        grads[step, 0] = jnp.where(flag_spot, update, own).astype(bf16)
        send(2 + step)
        if step == ITERS - 1:
            keep_own.start()
            keep_window.start()
            for phase in range(1 + ITERS):
                wait_sent(phase)
            keep_window.wait()
            keep_own.wait()
            for di, dj in DIRS:

                @pl.when(jnp.logical_not(exists(di, dj)))
                def _(di=di, dj=dj):
                    blank(di, dj).wait()
        if step == 0:
            wait_arrivals(1)
            for at in (0, 1):
                start = core + at * HALO
                window[start : start + HALO, :core] = whole_of(vert16[at], vert_rest[at])
            window[:, core:] = unpack(side16) + unpack(side_rest)
        wait_arrivals(2 + step)

        if step < ITERS - 1:
            spread = band_gradient(grads.at[step], blocks, rows_ref)
            total = jnp.dot(spread, cols_ref[...], preferred_element_type=f32)
            for gi, (start, size) in enumerate(bands(core)):
                at = slice(start, start + size)
                scale = flag_row(grads.at[step], gi, core)
                window[at, :] = jnp.clip(window[at, :] - STEP_SIZE * scale * total[at], -1.0, 1.0)
    wait_sent(1 + ITERS)


def body(axes, mask_field, resist_goal, kernels, colour, active):
    core = mask_field.shape[0]
    tile = core + 2 * HALO
    kerns = kernels.shape[0]
    tables = make_tables(core, tile)
    f32, bf16 = jnp.float32, jnp.bfloat16
    sources = [mask_field, resist_goal, kernels.reshape(kerns, 2 * FREQS, FREQS)]
    sources += [jnp.asarray(table) for table in tables.values()]
    hbm = pl.BlockSpec(memory_space=pltpu.HBM)
    smem = pl.BlockSpec(memory_space=pltpu.SMEM)
    window, last = pl.pallas_call(
        functools.partial(kernel, axes, len(sources)),
        out_shape=(
            jax.ShapeDtypeStruct((tile, tile), f32),
            jax.ShapeDtypeStruct((9, FREQS, 128), bf16),
        ),
        in_specs=[smem, smem] + [hbm] * len(sources),
        out_specs=(hbm, hbm),
        scratch_shapes=[pltpu.VMEM(source.shape, source.dtype) for source in sources]
        + [
            pltpu.VMEM((core, core), bf16),
            pltpu.VMEM((core, core), bf16),
            pltpu.VMEM((2, tile // 2, 128), bf16),
            pltpu.VMEM((2, tile // 2, 128), bf16),
            pltpu.VMEM((2, HALO, core), bf16),
            pltpu.VMEM((2, tile // 2, 128), bf16),
            pltpu.VMEM((2, HALO, core), bf16),
            pltpu.VMEM((2, tile // 2, 128), bf16),
            pltpu.VMEM((tile, tile), f32),
            pltpu.VMEM((tile, tile), bf16),
            pltpu.VMEM((ITERS, 9, FREQS, 128), bf16),
            pltpu.VMEM((384, 384), bf16),
            pltpu.VMEM((kerns, FREQS, 128), f32),
            pltpu.VMEM((kerns, FREQS, 128), f32),
            pltpu.VMEM((core, core), f32),
            pltpu.VMEM((256, kerns * 256), bf16),
            pltpu.VMEM((256, kerns * 256), bf16),
            pltpu.VMEM((core, core), f32),
            pltpu.VMEM((core, core), bf16),
            pltpu.SemaphoreType.DMA((2 + ITERS, 9)),
            pltpu.SemaphoreType.DMA((2 + ITERS, 9)),
            pltpu.SemaphoreType.DMA((len(sources),)),
            pltpu.SemaphoreType.DMA((10,)),
        ],
        compiler_params=pltpu.CompilerParams(
            collective_id=0, has_side_effects=True, vmem_limit_bytes=56 * 1024 * 1024
        ),
    )(
        colour,
        active,
        *sources,
    )
    finals = [last, sources[-2], sources[-1], window]
    return pl.pallas_call(
        finish,
        out_shape=(
            jax.ShapeDtypeStruct((core, core), f32),
            jax.ShapeDtypeStruct((tile, tile), f32),
        ),
        in_specs=[hbm] * len(finals),
        out_specs=(hbm, hbm),
        scratch_shapes=[pltpu.VMEM(source.shape, source.dtype) for source in finals]
        + [
            pltpu.VMEM((384, 384), bf16),
            pltpu.VMEM((core, core), f32),
            pltpu.VMEM((tile, tile), f32),
            pltpu.SemaphoreType.DMA((4,)),
            pltpu.SemaphoreType.DMA((4,)),
        ],
        compiler_params=pltpu.CompilerParams(vmem_limit_bytes=56 * 1024 * 1024),
    )(*finals)


def solution(mesh):
    axes = mesh.axis_names
    return jax.shard_map(
        functools.partial(body, axes),
        mesh=mesh,
        in_specs=(P(*axes), P(*axes), P(), P(*axes), P(*axes)),
        out_specs=(P(*axes), P(*axes)),
        check_vma=False,
    )
```
